32 devices in a mesh: gx: 4 (over y, core), gy: 8 (over z, x).
Axes of the slice: x: 2, y: 2, z: 4, core: 2. Of those that a mesh axis runs over, the one named last changes fastest.
Arguments:
- state: float32 [4, 128, 32, 1024], P(None, 'gx', 'gy'), may hold values from -8 to 8
- diffusivity: float32 [128, 32, 1024], P('gx', 'gy'), may hold values from 0.1 to 10
Outputs:
- state_next: float32 [4, 128, 32, 1024], P(None, 'gx', 'gy')
The draws below stay inside these ranges and needn't reach their ends.
All inputs are finite; a program needn't handle non-finite values.
Results may differ from the reference program's by a relative error of at most 0.0003.
Values sent between devices are 32-bit elements; how exact they have to be, the bound alone decides.
A program may use at most 64 MiB of HBM per device.

```python
import math
import jax
import jax.numpy as jnp
from jax import lax

NZ = 1024
NX = 128
NY = 32


def draw_state(key, part):
    keys = jax.random.split(jax.random.fold_in(key, 11), 2)
    rough = jax.random.normal(keys[0], (4, NX, NY, NZ), jnp.float32)
    amounts = jax.random.normal(keys[1], (4, 3, NY, NZ), jnp.float32)
    position = (jnp.arange(NX, dtype=jnp.float32) + 0.5) / NX
    orders = jnp.arange(1, 4, dtype=jnp.float32)
    modes = jnp.sin(jnp.pi * orders[:, None] * position[None, :])
    smooth = jnp.einsum('fmyz,mx->fxyz', amounts, modes)
    return jnp.clip(rough + smooth, -8.0, 8.0)


def block_scale(rng, shape, cuts, low, top_value):
    def one(dim, parts):
        heights = jax.random.uniform(jax.random.fold_in(jax.random.fold_in(rng, 6), dim), (parts,), jnp.float32, low / len(cuts), top_value / len(cuts))
        return jnp.repeat(jnp.exp(heights), shape[dim] // parts).reshape((-1,) + (1,) * (len(shape) - dim - 1))

    factor_of = one(*cuts[0])
    for cut in cuts[1:]:
        factor_of = factor_of * one(*cut)
    return factor_of


def setup_inputs(seed: int = 0) -> dict:
    arg_keys = jax.random.split(jax.random.key(seed), 3)
    return {
        "state": draw_state(jax.random.fold_in(arg_keys[2], 71), 0),
        "diffusivity": jnp.clip(jnp.exp(math.log(10.0) - 4.6051702 * jax.random.uniform(arg_keys[1], (NX, NY, NZ), jnp.float32) ** block_scale(arg_keys[1], (NX, NY, NZ), ((0, 4), (1, 8)), -0.2, 0.2)), 0.1, 10.0),
    }


diff_number = 4000.0
scalar_ratio = 1.4
step_size = 0.1


def along(field, axis):
    near = jnp.roll(field, -1, axis) - jnp.roll(field, 1, axis)
    far = jnp.roll(field, -2, axis) - jnp.roll(field, 2, axis)
    return (8.0 * near - far) / 12.0


def advect(plane):
    return -(plane[1:2] * along(plane, 1) + plane[2:3] * along(plane, 2))


def sections(plane):
    first = advect(plane)
    middle = plane + step_size * first
    return plane + 0.5 * step_size * (first + advect(middle))


def sweep(sub, main, sup, right_side):
    def down(carry, row):
        ratio_prev, value_prev = carry
        low, centre, upp, given = row
        pivot = centre - low * ratio_prev
        ratio = upp / pivot
        value = (given - low[None] * value_prev) / pivot[None]
        return (ratio, value), (ratio, value)

    start = (jnp.zeros(main.shape[1:], jnp.float32), jnp.zeros(right_side.shape[1:], jnp.float32))
    _, (ratios, values) = lax.scan(down, start, (sub, main, sup, right_side))

    def upward(after, row):
        ratio, value = row
        here = value - ratio[None] * after
        return here, here

    _, result = lax.scan(upward, jnp.zeros(right_side.shape[1:], jnp.float32), (ratios, values), reverse=True)
    return result


def line_solve(lower, upper, right_side):
    main = 1.0 + lower + upper
    zero_row = jnp.zeros_like(lower[:1])
    sub = jnp.concatenate([zero_row, -lower[1:]], 0)
    sup = jnp.concatenate([-upper[:-1], zero_row], 0)
    return sweep(sub, main, sup, right_side)


def implicit(pieces):
    rows, kappa = pieces
    zero_row = jnp.zeros_like(kappa[:1])
    padded = jnp.concatenate([zero_row, kappa, zero_row], 0)
    lower = 0.5 * diff_number * (padded[:-2] + padded[1:-1])
    upper = 0.5 * diff_number * (padded[1:-1] + padded[2:])
    flow = line_solve(lower, upper, rows[:, :3])
    heat = line_solve(scalar_ratio * lower, scalar_ratio * upper, rows[:, 3:])
    return jnp.concatenate([flow, heat], 1)


def reference(state, diffusivity):
    mixed = lax.map(sections, jnp.moveaxis(state, 1, 0))
    solved = lax.map(implicit, (jnp.moveaxis(mixed, 2, 0), jnp.moveaxis(diffusivity, 1, 0)))
    return jnp.transpose(solved, (2, 1, 0, 3))
```

```python
import functools

import jax
import jax.numpy as jnp
from jax import lax
from jax.experimental import pallas as pl
from jax.experimental.pallas import tpu as pltpu
from jax.sharding import PartitionSpec as P

diff_number = 4000.0
scalar_ratio = 1.4
step_size = 0.1
LANES = 128
MESH = pl.DeviceIdType.MESH


def along_z(v):
    lane = lax.broadcasted_iota(jnp.int32, v.shape, 2)
    subs = v.shape[1]
    up = pltpu.roll(v, subs - 1, 1)
    down = pltpu.roll(v, 1, 1)
    plus1 = pltpu.roll(jnp.where(lane < 1, up, v), LANES - 1, 2)
    plus2 = pltpu.roll(jnp.where(lane < 2, up, v), LANES - 2, 2)
    minus1 = pltpu.roll(jnp.where(lane >= LANES - 1, down, v), 1, 2)
    minus2 = pltpu.roll(jnp.where(lane >= LANES - 2, down, v), 2, 2)
    return (8.0 / 12.0) * (plus1 - minus1) - (1.0 / 12.0) * (plus2 - minus2)


def tendency(rows):
    n = rows[0].shape[0] - 4
    centre = [q[2 : 2 + n] for q in rows]
    out = []
    for q, mid in zip(rows, centre):
        near = q[3 : 3 + n] - q[1 : 1 + n]
        far = q[4 : 4 + n] - q[0:n]
        dy = (8.0 / 12.0) * near - (1.0 / 12.0) * far
        out.append(-(centre[1] * dy + centre[2] * along_z(mid)))
    return out, centre


def mixed_rows(rows):
    first, centre = tendency(rows)
    middle = [s + step_size * f for s, f in zip(centre, first)]
    second, _ = tendency(middle)
    n = second[0].shape[0]
    return [
        s[2 : 2 + n] + (0.5 * step_size) * (f[2 : 2 + n] + g)
        for s, f, g in zip(centre, first, second)
    ]


def kernel(
    gx,
    gy,
    chunks,
    rounds,
    state,
    kappa,
    out,
    halo,
    kside,
    coef,
    vprev,
    qacc,
    sum_m,
    sum_v,
    inv_d,
    track_b,
    track_c,
    take_s,
    take_e,
    edge,
    near_send,
    near_recv,
    far_send,
    far_recv,
    k_send,
    k_recv,
    m_send,
    m_recv,
    v_send,
    v_recv,
):
    pos = lax.axis_index("gx")
    g = lax.axis_index("gy")
    odd = lax.rem(g, 2)
    partner = g + 1 - 2 * odd
    ahead = lax.rem(g + 2 - 4 * odd + gy, gy)
    behind = lax.rem(g - 2 + 4 * odd + gy, gy)
    nx, ny = kappa.shape[0], kappa.shape[1]
    width = nx // chunks
    tile = kappa.shape[1:]

    barrier = pltpu.get_barrier_semaphore()
    for other in (partner, ahead, behind):
        pl.semaphore_signal(barrier, inc=1, device_id={"gy": other}, device_id_type=MESH)
    for j in range(1, gx):
        pl.semaphore_signal(
            barrier, inc=1, device_id={"gx": lax.rem(pos + j, gx)}, device_id_type=MESH
        )
    pl.semaphore_wait(barrier, 3 + gx - 1)

    def near(c):
        part = pl.ds(c * width, width)
        return pltpu.make_async_remote_copy(
            src_ref=state.at[:, part],
            dst_ref=halo.at[odd, :, part],
            send_sem=near_send.at[c],
            recv_sem=near_recv.at[c],
            device_id={"gy": partner},
            device_id_type=MESH,
        )

    def far(c):
        part = pl.ds(c * width, width)
        return pltpu.make_async_remote_copy(
            src_ref=halo.at[1 - odd, :, part],
            dst_ref=halo.at[odd, :, part],
            send_sem=far_send.at[c],
            recv_sem=far_recv.at[c],
            device_id={"gy": ahead},
            device_id_type=MESH,
        )

    def k_copy(to_right):
        return pltpu.make_async_remote_copy(
            src_ref=kappa.at[nx - 1 if to_right else 0],
            dst_ref=kside.at[0 if to_right else 1],
            send_sem=k_send.at[0 if to_right else 1],
            recv_sem=k_recv.at[0 if to_right else 1],
            device_id={"gx": lax.rem(pos + (1 if to_right else gx - 1), gx)},
            device_id_type=MESH,
        )

    def bit(k):
        return lax.rem(pos // (2**k), 2)

    def sums(buf, k, send, recv):
        b = bit(k)
        return pltpu.make_async_remote_copy(
            src_ref=buf.at[k, b],
            dst_ref=buf.at[k, b],
            send_sem=send.at[k],
            recv_sem=recv.at[k],
            device_id={"gx": pos + (2**k) * (1 - 2 * b)},
            device_id_type=MESH,
        )

    @pl.when(pos < gx - 1)
    def _():
        k_copy(True).start()

    @pl.when(pos > 0)
    def _():
        k_copy(False).start()

    @pl.loop(0, chunks)
    def _(c):
        near(c).start()

    zero = jnp.zeros(tile, jnp.float32)
    one = jnp.ones(tile, jnp.float32)

    @pl.when(pos > 0)
    def _():
        k_copy(True).wait_recv()

    @pl.when(pos < gx - 1)
    def _():
        k_copy(False).wait_recv()

    @pl.when(pos == 0)
    def _():
        kside[0] = zero

    @pl.when(pos == gx - 1)
    def _():
        kside[1] = zero

    scales = (0.5 * diff_number, 0.5 * diff_number * scalar_ratio)

    def matrix_row(i, k_before, k_here, k_after, carry):
        low_sum = k_before + k_here
        up_sum = k_here + k_after
        new = []
        for m, scale in enumerate(scales):
            slack, w, head_p, head_r = carry[m]
            low = scale * low_sum
            up = scale * up_sum
            excess = 1.0 + low * slack
            inv = 1.0 / (excess + up)
            ratio = up * inv
            linv = low * inv
            w = linv * w
            coef[m, 0, i] = ratio
            coef[m, 1, i] = w
            coef[m, 2, i] = inv
            coef[m, 3, i] = linv
            coef[m, 4, i] = head_p
            new.append((excess * inv, w, head_p * ratio, head_r + head_p * w))
        return tuple(new)

    carry = tuple((one, one, one, zero) for _ in scales)
    carry = matrix_row(0, kside[0], kappa[0], kappa[1], carry)
    carry = lax.fori_loop(
        1,
        nx - 1,
        lambda i, cr: matrix_row(i, kappa[i - 1], kappa[i], kappa[i + 1], cr),
        carry,
    )
    carry = matrix_row(nx - 1, kappa[nx - 2], kappa[nx - 1], kside[1], carry)
    for m in range(2):
        _, w, head_p, head_r = carry[m]
        b = bit(0)
        sum_m[0, b, m] = head_p
        sum_m[0, b, 2 + m] = head_r
        sum_m[0, b, 4 + m] = coef[m, 0, nx - 1]
        sum_m[0, b, 6 + m] = w
        track_b[0, m] = one
        track_c[0, m] = zero
        track_b[1, m] = zero
        track_c[1, m] = one
    if rounds:
        sums(sum_m, 0, m_send, m_recv).start()

    def merge_matrix(k):
        sums(sum_m, k, m_send, m_recv).wait_recv()
        b = bit(k)
        for m in range(2):
            p1, r1 = sum_m[k, 0, m], sum_m[k, 0, 2 + m]
            last1, w1 = sum_m[k, 0, 4 + m], sum_m[k, 0, 6 + m]
            p2, r2 = sum_m[k, 1, m], sum_m[k, 1, 2 + m]
            last2, w2 = sum_m[k, 1, 4 + m], sum_m[k, 1, 6 + m]
            inv = 1.0 / (1.0 - last1 * r2)
            inv_d[k, m] = inv
            end_b, end_c = w1 * inv, last1 * p2 * inv
            start_b, start_c = r2 * end_b, p2 + r2 * end_c
            if k + 1 < rounds:
                up = bit(k + 1)
                sum_m[k + 1, up, m] = p1 * start_c
                sum_m[k + 1, up, 2 + m] = r1 + p1 * start_b
                sum_m[k + 1, up, 4 + m] = last2 + w2 * end_c
                sum_m[k + 1, up, 6 + m] = w2 * end_b

            @pl.when(b == 0)
            def _():
                for side in range(2):
                    c = track_c[side, m]
                    take_s[k, side, m] = c
                    take_e[k, side, m] = zero
                    track_b[side, m] = track_b[side, m] + c * start_b
                    track_c[side, m] = c * start_c

            @pl.when(b == 1)
            def _():
                for side in range(2):
                    c = track_b[side, m]
                    take_s[k, side, m] = zero
                    take_e[k, side, m] = c
                    track_c[side, m] = track_c[side, m] + c * end_c
                    track_b[side, m] = c * end_b

        if k + 1 < rounds:
            sums(sum_m, k + 1, m_send, m_recv).start()

    near(0).wait_recv()
    far(0).start()
    for c in range(4):
        vprev[c] = zero
        qacc[c] = zero

    @pl.loop(0, chunks)
    def _(c):
        @pl.when(c + 1 < chunks)
        def _():
            near(c + 1).wait_recv()
            far(c + 1).start()

        for k in range(rounds):

            @pl.when(c == min(k, chunks - 1))
            def _():
                merge_matrix(k)

        far(c).wait_recv()

        @pl.loop(0, width)
        def _(j):
            x = c * width + j
            rows = [
                jnp.concatenate(
                    [halo[0, f, x][ny - 4 :], state[f, x], halo[1, f, x][:4]], 0
                )
                for f in range(4)
            ]
            mixed = mixed_rows(rows)
            for f in range(4):
                m = 1 if f == 3 else 0
                v = mixed[f] * coef[m, 2, x] + coef[m, 3, x] * vprev[f]
                vprev[f] = v
                out[f, x] = v
                qacc[f] = qacc[f] + coef[m, 4, x] * v

    for f in range(4):
        edge[0, f] = zero
        edge[1, f] = zero
    if rounds:
        b = bit(0)
        for f in range(4):
            sum_v[0, b, f] = qacc[f]
            sum_v[0, b, 4 + f] = vprev[f]
        sums(sum_v, 0, v_send, v_recv).start()
    for k in range(rounds):
        sums(sum_v, k, v_send, v_recv).wait_recv()
        for f in range(4):
            m = 1 if f == 3 else 0
            q1, v1 = sum_v[k, 0, f], sum_v[k, 0, 4 + f]
            q2, v2 = sum_v[k, 1, f], sum_v[k, 1, 4 + f]
            end_a = (v1 + sum_m[k, 0, 4 + m] * q2) * inv_d[k, m]
            start_a = q2 + sum_m[k, 1, 2 + m] * end_a
            if k + 1 < rounds:
                up = bit(k + 1)
                sum_v[k + 1, up, f] = q1 + sum_m[k, 0, m] * start_a
                sum_v[k + 1, up, 4 + f] = v2 + sum_m[k, 1, 6 + m] * end_a
            for side in range(2):
                edge[side, f] = (
                    edge[side, f] + take_s[k, side, m] * start_a + take_e[k, side, m] * end_a
                )
        if k + 1 < rounds:
            sums(sum_v, k + 1, v_send, v_recv).start()

    def upward(i, after):
        x = nx - 1 - i
        new = []
        for f in range(4):
            m = 1 if f == 3 else 0
            here = out[f, x] + coef[m, 1, x] * edge[0, f] + coef[m, 0, x] * after[f]
            out[f, x] = here
            new.append(here)
        return tuple(new)

    lax.fori_loop(0, nx, upward, tuple(edge[1, f] for f in range(4)))

    @pl.loop(0, chunks)
    def _(c):
        near(c).wait_send()
        far(c).wait_send()

    @pl.when(pos < gx - 1)
    def _():
        k_copy(True).wait_send()

    @pl.when(pos > 0)
    def _():
        k_copy(False).wait_send()

    for k in range(rounds):
        sums(sum_m, k, m_send, m_recv).wait_send()
        sums(sum_v, k, v_send, v_recv).wait_send()


def body(gx, gy, state, diffusivity):
    fields, nx, ny, nz = state.shape
    subs = nz // LANES
    tile = (ny, subs, LANES)
    rounds = gx.bit_length() - 1
    assert gx == 2**rounds and gy % 2 == 0 and ny >= 4
    chunks = 8 if nx % 8 == 0 else 1
    steps = max(rounds, 1)
    f32 = jnp.float32
    dma = pltpu.SemaphoreType.DMA
    call = pl.pallas_call(
        functools.partial(kernel, gx, gy, chunks, rounds),
        out_shape=jax.ShapeDtypeStruct((fields, nx) + tile, f32),
        in_specs=[pl.BlockSpec(memory_space=pltpu.VMEM)] * 2,
        out_specs=pl.BlockSpec(memory_space=pltpu.VMEM),
        scratch_shapes=[
            pltpu.VMEM((2, fields, nx) + tile, f32),
            pltpu.VMEM((2,) + tile, f32),
            pltpu.VMEM((2, 5, nx) + tile, f32),
            pltpu.VMEM((fields,) + tile, f32),
            pltpu.VMEM((fields,) + tile, f32),
            pltpu.VMEM((steps, 2, 8) + tile, f32),
            pltpu.VMEM((steps, 2, 8) + tile, f32),
            pltpu.VMEM((steps, 2) + tile, f32),
            pltpu.VMEM((2, 2) + tile, f32),
            pltpu.VMEM((2, 2) + tile, f32),
            pltpu.VMEM((steps, 2, 2) + tile, f32),
            pltpu.VMEM((steps, 2, 2) + tile, f32),
            pltpu.VMEM((2, fields) + tile, f32),
            dma((chunks,)),
            dma((chunks,)),
            dma((chunks,)),
            dma((chunks,)),
            dma((2,)),
            dma((2,)),
            dma((steps,)),
            dma((steps,)),
            dma((steps,)),
            dma((steps,)),
        ],
        compiler_params=pltpu.CompilerParams(
            collective_id=0, has_side_effects=True, vmem_limit_bytes=40 * 2**20
        ),
        cost_estimate=pl.CostEstimate(
            flops=100 * state.size, bytes_accessed=8 * state.size, transcendentals=0
        ),
    )
    result = call(state.reshape((fields, nx) + tile), diffusivity.reshape((nx,) + tile))
    return result.reshape(state.shape)


def solution(mesh):
    return jax.shard_map(
        functools.partial(body, mesh.shape["gx"], mesh.shape["gy"]),
        mesh=mesh,
        in_specs=(P(None, "gx", "gy", None), P("gx", "gy", None)),
        out_specs=P(None, "gx", "gy", None),
        check_vma=False,
    )
```

```python
import functools

import jax
import jax.numpy as jnp
from jax import lax
from jax.experimental import pallas as pl
from jax.experimental.pallas import tpu as pltpu
from jax.sharding import PartitionSpec as P

diff_number = 4000.0
scalar_ratio = 1.4
step_size = 0.1
LANES = 128
MESH = pl.DeviceIdType.MESH


def along_z(v):
    lane = lax.broadcasted_iota(jnp.int32, v.shape, 2)
    subs = v.shape[1]
    up = pltpu.roll(v, subs - 1, 1)
    down = pltpu.roll(v, 1, 1)
    plus1 = pltpu.roll(jnp.where(lane < 1, up, v), LANES - 1, 2)
    plus2 = pltpu.roll(jnp.where(lane < 2, up, v), LANES - 2, 2)
    minus1 = pltpu.roll(jnp.where(lane >= LANES - 1, down, v), 1, 2)
    minus2 = pltpu.roll(jnp.where(lane >= LANES - 2, down, v), 2, 2)
    return (8.0 / 12.0) * (plus1 - minus1) - (1.0 / 12.0) * (plus2 - minus2)


def along_y(q):
    n = q.shape[0] - 4
    near = q[3 : 3 + n] - q[1 : 1 + n]
    far = q[4 : 4 + n] - q[0:n]
    return (8.0 / 12.0) * near - (1.0 / 12.0) * far


def tendency(across, along, q):
    n = q.shape[0] - 4
    return -(across * along_y(q) + along * along_z(q[2 : 2 + n]))


PHASES = ((1, 2), (0,), (3,))


def kernel(
    gx,
    gy,
    ny,
    chunks,
    rounds,
    state,
    kappa,
    out,
    own,
    kap,
    halo,
    kside,
    coef,
    mid,
    vprev,
    qacc,
    sum_m,
    sum_v,
    inv_d,
    track_b,
    track_c,
    take_s,
    take_e,
    edge,
    own_sem,
    near_send,
    near_recv,
    far_send,
    far_recv,
    k_send,
    k_recv,
    m_send,
    m_recv,
    v_send,
    v_recv,
):
    pos = lax.axis_index("gx")
    g = lax.axis_index("gy")
    odd = lax.rem(g, 2)
    partner = g + 1 - 2 * odd
    ahead = lax.rem(g + 2 - 4 * odd + gy, gy)
    behind = lax.rem(g - 2 + 4 * odd + gy, gy)
    nx = kap.shape[0]
    width = nx // chunks
    tile = kap.shape[1:]
    subs = tile[0] // ny

    barrier = pltpu.get_barrier_semaphore()
    for other in (partner, ahead, behind):
        pl.semaphore_signal(barrier, inc=1, device_id={"gy": other}, device_id_type=MESH)
    for j in range(1, gx):
        pl.semaphore_signal(
            barrier, inc=1, device_id={"gx": lax.rem(pos + j, gx)}, device_id_type=MESH
        )

    def fields_of(ph):
        fields = PHASES[ph]
        return pl.ds(fields[0], len(fields))

    def own_copy(ph):
        f = fields_of(ph)
        return pltpu.make_async_copy(state.at[f], own.at[f], own_sem.at[ph])

    kap_copy = pltpu.make_async_copy(kappa, kap, own_sem.at[3])
    kap_copy.start()
    for ph in range(3):
        own_copy(ph).start()
    pl.semaphore_wait(barrier, 3 + gx - 1)

    def near(ph, c):
        f, part = fields_of(ph), pl.ds(c * width, width)
        return pltpu.make_async_remote_copy(
            src_ref=state.at[f, part],
            dst_ref=halo.at[odd, f, part],
            send_sem=near_send.at[ph, c],
            recv_sem=near_recv.at[ph, c],
            device_id={"gy": partner},
            device_id_type=MESH,
        )

    def far(ph, c):
        f, part = fields_of(ph), pl.ds(c * width, width)
        return pltpu.make_async_remote_copy(
            src_ref=halo.at[1 - odd, f, part],
            dst_ref=halo.at[odd, f, part],
            send_sem=far_send.at[ph, c],
            recv_sem=far_recv.at[ph, c],
            device_id={"gy": ahead},
            device_id_type=MESH,
        )

    def forward(ph, c):
        near(ph, c).wait_recv()
        far(ph, c).start()

    def k_copy(to_right):
        side = 0 if to_right else 1
        return pltpu.make_async_remote_copy(
            src_ref=kappa.at[nx - 1 if to_right else 0],
            dst_ref=kside.at[side],
            send_sem=k_send.at[side],
            recv_sem=k_recv.at[side],
            device_id={"gx": lax.rem(pos + (1 if to_right else gx - 1), gx)},
            device_id_type=MESH,
        )

    def bit(k):
        return lax.rem(pos // (2**k), 2)

    def m_copy(k):
        b = bit(k)
        return pltpu.make_async_remote_copy(
            src_ref=sum_m.at[k, b],
            dst_ref=sum_m.at[k, b],
            send_sem=m_send.at[k],
            recv_sem=m_recv.at[k],
            device_id={"gx": pos + (2**k) * (1 - 2 * b)},
            device_id_type=MESH,
        )

    def v_copy(ph, k):
        b = bit(k)
        part = pl.ds(0, 2 * len(PHASES[ph]))
        return pltpu.make_async_remote_copy(
            src_ref=sum_v.at[ph, k, b, part],
            dst_ref=sum_v.at[ph, k, b, part],
            send_sem=v_send.at[ph, k],
            recv_sem=v_recv.at[ph, k],
            device_id={"gx": pos + (2**k) * (1 - 2 * b)},
            device_id_type=MESH,
        )

    @pl.when(pos < gx - 1)
    def _():
        k_copy(True).start()

    @pl.when(pos > 0)
    def _():
        k_copy(False).start()

    for ph in range(3):

        @pl.loop(0, chunks)
        def _(c):
            near(ph, c).start()

    zero = jnp.zeros(tile, jnp.float32)
    one = jnp.ones(tile, jnp.float32)
    kap_copy.wait()

    @pl.when(pos > 0)
    def _():
        k_copy(True).wait_recv()

    @pl.when(pos < gx - 1)
    def _():
        k_copy(False).wait_recv()

    @pl.when(pos == 0)
    def _():
        kside[0] = zero

    @pl.when(pos == gx - 1)
    def _():
        kside[1] = zero

    scales = (0.5 * diff_number, 0.5 * diff_number * scalar_ratio)

    def matrix_row(i, k_before, k_here, k_after, carry):
        low_sum = k_before + k_here
        up_sum = k_here + k_after
        new = []
        for m, scale in enumerate(scales):
            slack, w, head_p, head_r = carry[m]
            low = scale * low_sum
            up = scale * up_sum
            excess = 1.0 + low * slack
            inv = 1.0 / (excess + up)
            ratio = up * inv
            linv = low * inv
            w = linv * w
            coef[m, 0, i] = ratio
            coef[m, 1, i] = w
            coef[m, 2, i] = inv
            coef[m, 3, i] = linv
            coef[m, 4, i] = head_p
            new.append((excess * inv, w, head_p * ratio, head_r + head_p * w))
        return tuple(new)

    carry = tuple((one, one, one, zero) for _ in scales)
    carry = matrix_row(0, kside[0], kap[0], kap[1], carry)
    carry = lax.fori_loop(
        1,
        nx - 1,
        lambda i, cr: matrix_row(i, kap[i - 1], kap[i], kap[i + 1], cr),
        carry,
    )
    carry = matrix_row(nx - 1, kap[nx - 2], kap[nx - 1], kside[1], carry)
    for m in range(2):
        _, w, head_p, head_r = carry[m]
        b = bit(0)
        sum_m[0, b, m] = head_p
        sum_m[0, b, 2 + m] = head_r
        sum_m[0, b, 4 + m] = coef[m, 0, nx - 1]
        sum_m[0, b, 6 + m] = w
        track_b[0, m] = one
        track_c[0, m] = zero
        track_b[1, m] = zero
        track_c[1, m] = one
    if rounds:
        m_copy(0).start()

    def merge_matrix(k):
        m_copy(k).wait_recv()
        b = bit(k)
        for m in range(2):
            p1, r1 = sum_m[k, 0, m], sum_m[k, 0, 2 + m]
            last1, w1 = sum_m[k, 0, 4 + m], sum_m[k, 0, 6 + m]
            p2, r2 = sum_m[k, 1, m], sum_m[k, 1, 2 + m]
            last2, w2 = sum_m[k, 1, 4 + m], sum_m[k, 1, 6 + m]
            inv = 1.0 / (1.0 - last1 * r2)
            inv_d[k, m] = inv
            end_b, end_c = w1 * inv, last1 * p2 * inv
            start_b, start_c = r2 * end_b, p2 + r2 * end_c
            if k + 1 < rounds:
                up = bit(k + 1)
                sum_m[k + 1, up, m] = p1 * start_c
                sum_m[k + 1, up, 2 + m] = r1 + p1 * start_b
                sum_m[k + 1, up, 4 + m] = last2 + w2 * end_c
                sum_m[k + 1, up, 6 + m] = w2 * end_b

            @pl.when(b == 0)
            def _():
                for side in range(2):
                    c = track_c[side, m]
                    take_s[k, side, m] = c
                    take_e[k, side, m] = zero
                    track_b[side, m] = track_b[side, m] + c * start_b
                    track_c[side, m] = c * start_c

            @pl.when(b == 1)
            def _():
                for side in range(2):
                    c = track_b[side, m]
                    take_s[k, side, m] = zero
                    take_e[k, side, m] = c
                    track_c[side, m] = track_c[side, m] + c * end_c
                    track_b[side, m] = c * end_b

        if k + 1 < rounds:
            m_copy(k + 1).start()

    def matrix_of(f):
        return 1 if f == 3 else 0

    def start_values(ph):
        b = bit(0)
        for j, f in enumerate(PHASES[ph]):
            sum_v[ph, 0, b, 2 * j] = qacc[f]
            sum_v[ph, 0, b, 2 * j + 1] = vprev[f]
        v_copy(ph, 0).start()

    def merge_values(ph, k):
        v_copy(ph, k).wait_recv()
        for j, f in enumerate(PHASES[ph]):
            m = matrix_of(f)
            q1, v1 = sum_v[ph, k, 0, 2 * j], sum_v[ph, k, 0, 2 * j + 1]
            q2, v2 = sum_v[ph, k, 1, 2 * j], sum_v[ph, k, 1, 2 * j + 1]
            end_a = (v1 + sum_m[k, 0, 4 + m] * q2) * inv_d[k, m]
            start_a = q2 + sum_m[k, 1, 2 + m] * end_a
            if k + 1 < rounds:
                up = bit(k + 1)
                sum_v[ph, k + 1, up, 2 * j] = q1 + sum_m[k, 0, m] * start_a
                sum_v[ph, k + 1, up, 2 * j + 1] = v2 + sum_m[k, 1, 6 + m] * end_a
            for side in range(2):
                edge[side, f] = (
                    edge[side, f] + take_s[k, side, m] * start_a + take_e[k, side, m] * end_a
                )
        if k + 1 < rounds:
            v_copy(ph, k + 1).start()

    def substitute(ph):
        fields = PHASES[ph]
        lefts = tuple(edge[0, f] for f in fields)

        def upward(i, after):
            x = nx - 1 - i
            new = []
            for f, left, nxt in zip(fields, lefts, after):
                m = matrix_of(f)
                here = out[f, x] + coef[m, 1, x] * left + coef[m, 0, x] * nxt
                out[f, x] = here
                new.append(here)
            return tuple(new)

        lax.fori_loop(0, nx, upward, tuple(edge[1, f] for f in fields))

    def rows_of(f, x, reach):
        def row(ref, y):
            return ref[x, pl.ds(y, subs, stride=ny), :]

        return jnp.stack(
            [row(halo.at[0, f], y) for y in range(ny - reach, ny)]
            + [row(own.at[f], y) for y in range(ny)]
            + [row(halo.at[1, f], y) for y in range(reach)]
        )

    def advect(ph, x):
        fields = PHASES[ph]
        wide = [rows_of(f, x, 4) for f in fields]
        if ph == 0:
            across, along = (q[2 : 6 + ny] for q in wide)
        else:
            across, along = rows_of(1, x, 2), rows_of(2, x, 2)
        firsts = [tendency(across, along, q) for q in wide]
        middles = [q[2 : 6 + ny] + step_size * t for q, t in zip(wide, firsts)]
        if ph == 0:
            mid_across, mid_along = (q[2 : 2 + ny] for q in middles)
            mid[0, x] = mid_across
            mid[1, x] = mid_along
        else:
            mid_across, mid_along = mid[0, x], mid[1, x]
        for f, q, t, p in zip(fields, wide, firsts, middles):
            second = tendency(mid_across, mid_along, p)
            mixed = q[4 : 4 + ny] + (0.5 * step_size) * (t[2 : 2 + ny] + second)
            for y in range(ny):
                out[f, x, pl.ds(y, subs, stride=ny), :] = mixed[y]

    def eliminate(f, begin):
        m = matrix_of(f)

        def down(j, carry):
            v, q = carry
            x = begin + j
            v = out[f, x] * coef[m, 2, x] + coef[m, 3, x] * v
            out[f, x] = v
            return v, q + coef[m, 4, x] * v

        v, q = lax.fori_loop(0, width, down, (vprev[f], qacc[f]))
        vprev[f] = v
        qacc[f] = q

    ahead_by = min(2, chunks)
    for c in range(ahead_by):
        forward(0, c)
    for f in range(4):
        vprev[f] = zero
        qacc[f] = zero
        edge[0, f] = zero
        edge[1, f] = zero

    for ph in range(3):
        own_copy(ph).wait()

        @pl.loop(0, chunks)
        def _(c):
            @pl.when(c + ahead_by < chunks)
            def _():
                forward(ph, c + ahead_by)

            if ph < 2:

                @pl.when(c + ahead_by >= chunks)
                def _():
                    forward(ph + 1, c + ahead_by - chunks)

            for k in range(rounds):
                if ph == 0:

                    @pl.when(c == min(k, chunks - 1))
                    def _():
                        merge_matrix(k)

                else:

                    @pl.when(c == min(2 * k + 2, chunks - 1))
                    def _():
                        merge_values(ph - 1, k)

            if ph > 0:

                @pl.when(c == min(2 * rounds + 2, chunks - 1))
                def _():
                    substitute(ph - 1)

            far(ph, c).wait_recv()

            @pl.loop(0, width)
            def _(j):
                advect(ph, c * width + j)

            for f in PHASES[ph]:
                eliminate(f, c * width)

        if rounds:
            start_values(ph)

    for k in range(rounds):
        merge_values(2, k)
    substitute(2)

    for ph in range(3):

        @pl.loop(0, chunks)
        def _(c):
            near(ph, c).wait_send()
            far(ph, c).wait_send()

    @pl.when(pos < gx - 1)
    def _():
        k_copy(True).wait_send()

    @pl.when(pos > 0)
    def _():
        k_copy(False).wait_send()

    for k in range(rounds):
        m_copy(k).wait_send()
        for ph in range(3):
            v_copy(ph, k).wait_send()


def flat(a):
    *lead, ny, nz = a.shape
    a = a.reshape(*lead, ny, nz // LANES, LANES)
    return jnp.swapaxes(a, -3, -2).reshape(*lead, ny * nz // LANES, LANES)


def body(gx, gy, state, diffusivity):
    fields, nx, ny, nz = state.shape
    subs = nz // LANES
    tile = (ny * subs, LANES)
    rounds = gx.bit_length() - 1
    assert gx == 2**rounds and gy % 2 == 0 and ny >= 4
    chunks = 8 if nx % 8 == 0 else 1
    steps = max(rounds, 1)
    f32 = jnp.float32
    dma = pltpu.SemaphoreType.DMA
    call = pl.pallas_call(
        functools.partial(kernel, gx, gy, ny, chunks, rounds),
        out_shape=jax.ShapeDtypeStruct((fields, nx) + tile, f32),
        in_specs=[pl.BlockSpec(memory_space=pltpu.HBM)] * 2,
        out_specs=pl.BlockSpec(memory_space=pltpu.VMEM),
        scratch_shapes=[
            pltpu.VMEM((fields, nx) + tile, f32),
            pltpu.VMEM((nx,) + tile, f32),
            pltpu.VMEM((2, fields, nx) + tile, f32),
            pltpu.VMEM((2,) + tile, f32),
            pltpu.VMEM((2, 5, nx) + tile, f32),
            pltpu.VMEM((2, nx, ny, subs, LANES), f32),
            pltpu.VMEM((fields,) + tile, f32),
            pltpu.VMEM((fields,) + tile, f32),
            pltpu.VMEM((steps, 2, 8) + tile, f32),
            pltpu.VMEM((3, steps, 2, 4) + tile, f32),
            pltpu.VMEM((steps, 2) + tile, f32),
            pltpu.VMEM((2, 2) + tile, f32),
            pltpu.VMEM((2, 2) + tile, f32),
            pltpu.VMEM((steps, 2, 2) + tile, f32),
            pltpu.VMEM((steps, 2, 2) + tile, f32),
            pltpu.VMEM((2, fields) + tile, f32),
            dma((4,)),
            dma((3, chunks)),
            dma((3, chunks)),
            dma((3, chunks)),
            dma((3, chunks)),
            dma((2,)),
            dma((2,)),
            dma((steps,)),
            dma((steps,)),
            dma((3, steps)),
            dma((3, steps)),
        ],
        compiler_params=pltpu.CompilerParams(
            collective_id=0, has_side_effects=True, vmem_limit_bytes=62 * 2**20
        ),
        cost_estimate=pl.CostEstimate(
            flops=100 * state.size, bytes_accessed=8 * state.size, transcendentals=0
        ),
    )
    result = call(flat(state), flat(diffusivity)).reshape(fields, nx, subs, ny, LANES)
    return jnp.swapaxes(result, -3, -2).reshape(state.shape)


def solution(mesh):
    return jax.shard_map(
        functools.partial(body, mesh.shape["gx"], mesh.shape["gy"]),
        mesh=mesh,
        in_specs=(P(None, "gx", "gy", None), P("gx", "gy", None)),
        out_specs=P(None, "gx", "gy", None),
        check_vma=False,
    )
```

```python
import functools

import jax
import jax.numpy as jnp
from jax import lax
from jax.experimental import pallas as pl
from jax.experimental.pallas import tpu as pltpu
from jax.sharding import PartitionSpec as P

diff_number = 4000.0
scalar_ratio = 1.4
step_size = 0.1
LANES = 128
MESH = pl.DeviceIdType.MESH


def along_z(q):
    v = q.reshape((-1,) + q.shape[-2:])
    lane = lax.broadcasted_iota(jnp.int32, v.shape, 2)
    subs = v.shape[1]
    up = pltpu.roll(v, subs - 1, 1)
    down = pltpu.roll(v, 1, 1)
    plus1 = pltpu.roll(jnp.where(lane < 1, up, v), LANES - 1, 2)
    plus2 = pltpu.roll(jnp.where(lane < 2, up, v), LANES - 2, 2)
    minus1 = pltpu.roll(jnp.where(lane >= LANES - 1, down, v), 1, 2)
    minus2 = pltpu.roll(jnp.where(lane >= LANES - 2, down, v), 2, 2)
    change = (8.0 / 12.0) * (plus1 - minus1) - (1.0 / 12.0) * (plus2 - minus2)
    return change.reshape(q.shape)


def along_y(q):
    n = q.shape[0] - 4
    near = q[3 : 3 + n] - q[1 : 1 + n]
    far = q[4 : 4 + n] - q[0:n]
    return (8.0 / 12.0) * near - (1.0 / 12.0) * far


def tendency(across, along, q):
    n = q.shape[0] - 4
    return -(across * along_y(q) + along * along_z(q[2 : 2 + n]))


PHASES = ((1, 2), (0,), (3,))


def kernel(
    gx,
    gy,
    ny,
    chunks,
    rounds,
    state,
    kappa,
    out,
    own,
    kap,
    halo,
    kside,
    coef,
    mid,
    vprev,
    qacc,
    sum_m,
    sum_v,
    inv_d,
    track_b,
    track_c,
    take_s,
    take_e,
    edge,
    own_sem,
    near_send,
    near_recv,
    far_send,
    far_recv,
    k_send,
    k_recv,
    m_send,
    m_recv,
    v_send,
    v_recv,
):
    pos = lax.axis_index("gx")
    g = lax.axis_index("gy")
    odd = lax.rem(g, 2)
    partner = g + 1 - 2 * odd
    ahead = lax.rem(g + 2 - 4 * odd + gy, gy)
    behind = lax.rem(g - 2 + 4 * odd + gy, gy)
    nx = kap.shape[0]
    width = nx // chunks
    tile = kap.shape[1:]
    subs = tile[0] // ny

    barrier = pltpu.get_barrier_semaphore()
    for other in (partner, ahead, behind):
        pl.semaphore_signal(barrier, inc=1, device_id={"gy": other}, device_id_type=MESH)
    for j in range(1, gx):
        pl.semaphore_signal(
            barrier, inc=1, device_id={"gx": lax.rem(pos + j, gx)}, device_id_type=MESH
        )

    def fields_of(ph):
        fields = PHASES[ph]
        return pl.ds(fields[0], len(fields))

    def own_copy(ph):
        f = fields_of(ph)
        return pltpu.make_async_copy(state.at[f], own.at[f], own_sem.at[ph])

    kap_copy = pltpu.make_async_copy(kappa, kap, own_sem.at[3])
    kap_copy.start()
    for ph in range(3):
        own_copy(ph).start()
    pl.semaphore_wait(barrier, 3 + gx - 1)

    def near(ph, c):
        f, part = fields_of(ph), pl.ds(c * width, width)
        return pltpu.make_async_remote_copy(
            src_ref=state.at[f, part],
            dst_ref=halo.at[odd, f, part],
            send_sem=near_send.at[ph, c],
            recv_sem=near_recv.at[ph, c],
            device_id={"gy": partner},
            device_id_type=MESH,
        )

    def far(ph, c):
        f, part = fields_of(ph), pl.ds(c * width, width)
        return pltpu.make_async_remote_copy(
            src_ref=halo.at[1 - odd, f, part],
            dst_ref=halo.at[odd, f, part],
            send_sem=far_send.at[ph, c],
            recv_sem=far_recv.at[ph, c],
            device_id={"gy": ahead},
            device_id_type=MESH,
        )

    def forward(ph, c):
        near(ph, c).wait_recv()
        far(ph, c).start()

    def k_copy(to_right):
        side = 0 if to_right else 1
        return pltpu.make_async_remote_copy(
            src_ref=kappa.at[nx - 1 if to_right else 0],
            dst_ref=kside.at[side],
            send_sem=k_send.at[side],
            recv_sem=k_recv.at[side],
            device_id={"gx": lax.rem(pos + (1 if to_right else gx - 1), gx)},
            device_id_type=MESH,
        )

    def bit(k):
        return lax.rem(pos // (2**k), 2)

    def m_copy(k):
        b = bit(k)
        return pltpu.make_async_remote_copy(
            src_ref=sum_m.at[k, b],
            dst_ref=sum_m.at[k, b],
            send_sem=m_send.at[k],
            recv_sem=m_recv.at[k],
            device_id={"gx": pos + (2**k) * (1 - 2 * b)},
            device_id_type=MESH,
        )

    def v_copy(ph, k):
        b = bit(k)
        part = pl.ds(0, 2 * len(PHASES[ph]))
        return pltpu.make_async_remote_copy(
            src_ref=sum_v.at[ph, k, b, part],
            dst_ref=sum_v.at[ph, k, b, part],
            send_sem=v_send.at[ph, k],
            recv_sem=v_recv.at[ph, k],
            device_id={"gx": pos + (2**k) * (1 - 2 * b)},
            device_id_type=MESH,
        )

    @pl.when(pos < gx - 1)
    def _():
        k_copy(True).start()

    @pl.when(pos > 0)
    def _():
        k_copy(False).start()

    for ph in range(3):

        @pl.loop(0, chunks)
        def _(c):
            near(ph, c).start()

    zero = jnp.zeros(tile, jnp.float32)
    one = jnp.ones(tile, jnp.float32)
    kap_copy.wait()

    @pl.when(pos > 0)
    def _():
        k_copy(True).wait_recv()

    @pl.when(pos < gx - 1)
    def _():
        k_copy(False).wait_recv()

    @pl.when(pos == 0)
    def _():
        kside[0] = zero

    @pl.when(pos == gx - 1)
    def _():
        kside[1] = zero

    scales = (0.5 * diff_number, 0.5 * diff_number * scalar_ratio)

    def matrix_row(i, k_before, k_here, k_after, carry):
        low_sum = k_before + k_here
        up_sum = k_here + k_after
        new = []
        for m, scale in enumerate(scales):
            slack, w, head_p, head_r = carry[m]
            low = scale * low_sum
            up = scale * up_sum
            excess = 1.0 + low * slack
            inv = 1.0 / (excess + up)
            ratio = up * inv
            linv = low * inv
            w = linv * w
            coef[m, 0, i] = ratio
            coef[m, 1, i] = w
            coef[m, 2, i] = inv
            coef[m, 3, i] = linv
            coef[m, 4, i] = head_p
            new.append((excess * inv, w, head_p * ratio, head_r + head_p * w))
        return tuple(new)

    carry = tuple((one, one, one, zero) for _ in scales)
    carry = matrix_row(0, kside[0], kap[0], kap[1], carry)
    ahead_by = min(2, chunks)
    begin = 1
    for c in range(ahead_by + 1):
        until = (nx - 1) * (c + 1) // (ahead_by + 1)
        carry = lax.fori_loop(
            begin,
            until,
            lambda i, cr: matrix_row(i, kap[i - 1], kap[i], kap[i + 1], cr),
            carry,
        )
        begin = until
        if c < ahead_by:
            forward(0, c)
    carry = matrix_row(nx - 1, kap[nx - 2], kap[nx - 1], kside[1], carry)
    for m in range(2):
        _, w, head_p, head_r = carry[m]
        b = bit(0)
        sum_m[0, b, m] = head_p
        sum_m[0, b, 2 + m] = head_r
        sum_m[0, b, 4 + m] = coef[m, 0, nx - 1]
        sum_m[0, b, 6 + m] = w
        track_b[0, m] = one
        track_c[0, m] = zero
        track_b[1, m] = zero
        track_c[1, m] = one
    if rounds:
        m_copy(0).start()

    def merge_matrix(k):
        m_copy(k).wait_recv()
        b = bit(k)
        for m in range(2):
            p1, r1 = sum_m[k, 0, m], sum_m[k, 0, 2 + m]
            last1, w1 = sum_m[k, 0, 4 + m], sum_m[k, 0, 6 + m]
            p2, r2 = sum_m[k, 1, m], sum_m[k, 1, 2 + m]
            last2, w2 = sum_m[k, 1, 4 + m], sum_m[k, 1, 6 + m]
            inv = 1.0 / (1.0 - last1 * r2)
            inv_d[k, m] = inv
            end_b, end_c = w1 * inv, last1 * p2 * inv
            start_b, start_c = r2 * end_b, p2 + r2 * end_c
            if k + 1 < rounds:
                up = bit(k + 1)
                sum_m[k + 1, up, m] = p1 * start_c
                sum_m[k + 1, up, 2 + m] = r1 + p1 * start_b
                sum_m[k + 1, up, 4 + m] = last2 + w2 * end_c
                sum_m[k + 1, up, 6 + m] = w2 * end_b

            @pl.when(b == 0)
            def _():
                for side in range(2):
                    c = track_c[side, m]
                    take_s[k, side, m] = c
                    take_e[k, side, m] = zero
                    track_b[side, m] = track_b[side, m] + c * start_b
                    track_c[side, m] = c * start_c

            @pl.when(b == 1)
            def _():
                for side in range(2):
                    c = track_b[side, m]
                    take_s[k, side, m] = zero
                    take_e[k, side, m] = c
                    track_c[side, m] = track_c[side, m] + c * end_c
                    track_b[side, m] = c * end_b

        if k + 1 < rounds:
            m_copy(k + 1).start()

    def matrix_of(f):
        return 1 if f == 3 else 0

    def start_values(ph):
        b = bit(0)
        for j, f in enumerate(PHASES[ph]):
            sum_v[ph, 0, b, 2 * j] = qacc[f]
            sum_v[ph, 0, b, 2 * j + 1] = vprev[f]
        v_copy(ph, 0).start()

    def merge_values(ph, k):
        v_copy(ph, k).wait_recv()
        for j, f in enumerate(PHASES[ph]):
            m = matrix_of(f)
            q1, v1 = sum_v[ph, k, 0, 2 * j], sum_v[ph, k, 0, 2 * j + 1]
            q2, v2 = sum_v[ph, k, 1, 2 * j], sum_v[ph, k, 1, 2 * j + 1]
            end_a = (v1 + sum_m[k, 0, 4 + m] * q2) * inv_d[k, m]
            start_a = q2 + sum_m[k, 1, 2 + m] * end_a
            if k + 1 < rounds:
                up = bit(k + 1)
                sum_v[ph, k + 1, up, 2 * j] = q1 + sum_m[k, 0, m] * start_a
                sum_v[ph, k + 1, up, 2 * j + 1] = v2 + sum_m[k, 1, 6 + m] * end_a
            for side in range(2):
                edge[side, f] = (
                    edge[side, f] + take_s[k, side, m] * start_a + take_e[k, side, m] * end_a
                )
        if k + 1 < rounds:
            v_copy(ph, k + 1).start()

    def substitute(ph):
        fields = PHASES[ph]
        lefts = tuple(edge[0, f] for f in fields)

        def upward(i, after):
            x = nx - 1 - i
            new = []
            for f, left, nxt in zip(fields, lefts, after):
                m = matrix_of(f)
                here = out[f, x] + coef[m, 1, x] * left + coef[m, 0, x] * nxt
                out[f, x] = here
                new.append(here)
            return tuple(new)

        lax.fori_loop(0, nx, upward, tuple(edge[1, f] for f in fields))

    def rows_of(f, part, reach):
        def row(ref, y):
            return ref[part, pl.ds(y, subs, stride=ny), :]

        return jnp.stack(
            [row(halo.at[0, f], y) for y in range(ny - reach, ny)]
            + [row(own.at[f], y) for y in range(ny)]
            + [row(halo.at[1, f], y) for y in range(reach)]
        )

    def advect(ph, part):
        fields = PHASES[ph]
        wide = [rows_of(f, part, 4) for f in fields]
        if ph == 0:
            across, along = (q[2 : 6 + ny] for q in wide)
        else:
            across, along = rows_of(1, part, 2), rows_of(2, part, 2)
        firsts = [tendency(across, along, q) for q in wide]
        middles = [q[2 : 6 + ny] + step_size * t for q, t in zip(wide, firsts)]
        if ph == 0:
            mid_across, mid_along = (q[2 : 2 + ny] for q in middles)
            mid[0, :, part] = mid_across
            mid[1, :, part] = mid_along
        else:
            mid_across, mid_along = mid[0, :, part], mid[1, :, part]
        for f, q, t, p in zip(fields, wide, firsts, middles):
            second = tendency(mid_across, mid_along, p)
            mixed = q[4 : 4 + ny] + (0.5 * step_size) * (t[2 : 2 + ny] + second)
            for y in range(ny):
                out[f, part, pl.ds(y, subs, stride=ny), :] = mixed[y]

    def eliminate(f, begin):
        m = matrix_of(f)

        def down(j, carry):
            v, q = carry
            x = begin + j
            v = out[f, x] * coef[m, 2, x] + coef[m, 3, x] * v
            out[f, x] = v
            return v, q + coef[m, 4, x] * v

        v, q = lax.fori_loop(0, width, down, (vprev[f], qacc[f]))
        vprev[f] = v
        qacc[f] = q

    for f in range(4):
        vprev[f] = zero
        qacc[f] = zero
        edge[0, f] = zero
        edge[1, f] = zero

    for ph in range(3):
        own_copy(ph).wait()

        @pl.loop(0, chunks)
        def _(c):
            @pl.when(c + ahead_by < chunks)
            def _():
                forward(ph, c + ahead_by)

            if ph < 2:

                @pl.when(c + ahead_by >= chunks)
                def _():
                    forward(ph + 1, c + ahead_by - chunks)

            for k in range(rounds):
                if ph == 0:

                    @pl.when(c == min(k, chunks - 1))
                    def _():
                        merge_matrix(k)

                else:

                    @pl.when(c == min(2 * k + 2, chunks - 1))
                    def _():
                        merge_values(ph - 1, k)

            if ph > 0:

                @pl.when(c == min(2 * rounds + 2, chunks - 1))
                def _():
                    substitute(ph - 1)

            far(ph, c).wait_recv()

            advect(ph, pl.ds(c * width, width))

            for f in PHASES[ph]:
                eliminate(f, c * width)

        if rounds:
            start_values(ph)

    for k in range(rounds):
        merge_values(2, k)
    substitute(2)

    for ph in range(3):

        @pl.loop(0, chunks)
        def _(c):
            near(ph, c).wait_send()
            far(ph, c).wait_send()

    @pl.when(pos < gx - 1)
    def _():
        k_copy(True).wait_send()

    @pl.when(pos > 0)
    def _():
        k_copy(False).wait_send()

    for k in range(rounds):
        m_copy(k).wait_send()
        for ph in range(3):
            v_copy(ph, k).wait_send()


def flat(a):
    *lead, ny, nz = a.shape
    a = a.reshape(*lead, ny, nz // LANES, LANES)
    return jnp.swapaxes(a, -3, -2).reshape(*lead, ny * nz // LANES, LANES)


def body(gx, gy, state, diffusivity):
    fields, nx, ny, nz = state.shape
    subs = nz // LANES
    tile = (ny * subs, LANES)
    rounds = gx.bit_length() - 1
    assert gx == 2**rounds and gy % 2 == 0 and ny >= 4
    chunks = 8 if nx % 8 == 0 else 1
    steps = max(rounds, 1)
    f32 = jnp.float32
    dma = pltpu.SemaphoreType.DMA
    call = pl.pallas_call(
        functools.partial(kernel, gx, gy, ny, chunks, rounds),
        out_shape=jax.ShapeDtypeStruct((fields, nx) + tile, f32),
        in_specs=[pl.BlockSpec(memory_space=pltpu.HBM)] * 2,
        out_specs=pl.BlockSpec(memory_space=pltpu.VMEM),
        scratch_shapes=[
            pltpu.VMEM((fields, nx) + tile, f32),
            pltpu.VMEM((nx,) + tile, f32),
            pltpu.VMEM((2, fields, nx) + tile, f32),
            pltpu.VMEM((2,) + tile, f32),
            pltpu.VMEM((2, 5, nx) + tile, f32),
            pltpu.VMEM((2, ny, nx, subs, LANES), f32),
            pltpu.VMEM((fields,) + tile, f32),
            pltpu.VMEM((fields,) + tile, f32),
            pltpu.VMEM((steps, 2, 8) + tile, f32),
            pltpu.VMEM((3, steps, 2, 4) + tile, f32),
            pltpu.VMEM((steps, 2) + tile, f32),
            pltpu.VMEM((2, 2) + tile, f32),
            pltpu.VMEM((2, 2) + tile, f32),
            pltpu.VMEM((steps, 2, 2) + tile, f32),
            pltpu.VMEM((steps, 2, 2) + tile, f32),
            pltpu.VMEM((2, fields) + tile, f32),
            dma((4,)),
            dma((3, chunks)),
            dma((3, chunks)),
            dma((3, chunks)),
            dma((3, chunks)),
            dma((2,)),
            dma((2,)),
            dma((steps,)),
            dma((steps,)),
            dma((3, steps)),
            dma((3, steps)),
        ],
        compiler_params=pltpu.CompilerParams(
            collective_id=0, has_side_effects=True, vmem_limit_bytes=62 * 2**20
        ),
        cost_estimate=pl.CostEstimate(
            flops=100 * state.size, bytes_accessed=8 * state.size, transcendentals=0
        ),
    )
    result = call(flat(state), flat(diffusivity)).reshape(fields, nx, subs, ny, LANES)
    return jnp.swapaxes(result, -3, -2).reshape(state.shape)


def solution(mesh):
    return jax.shard_map(
        functools.partial(body, mesh.shape["gx"], mesh.shape["gy"]),
        mesh=mesh,
        in_specs=(P(None, "gx", "gy", None), P("gx", "gy", None)),
        out_specs=P(None, "gx", "gy", None),
        check_vma=False,
    )
```

```python
import functools
import math

import jax
import jax.numpy as jnp
from jax import lax
from jax.experimental import pallas as pl
from jax.experimental.pallas import tpu as pltpu
from jax.sharding import PartitionSpec as P

diff_number = 4000.0
scalar_ratio = 1.4
step_size = 0.1
LANES = 128
MESH = pl.DeviceIdType.MESH


def along_z(q):
    v = q.reshape((-1,) + q.shape[-2:])
    lane = lax.broadcasted_iota(jnp.int32, v.shape, 2)
    subs = v.shape[1]
    up = pltpu.roll(v, subs - 1, 1)
    down = pltpu.roll(v, 1, 1)
    plus1 = pltpu.roll(jnp.where(lane < 1, up, v), LANES - 1, 2)
    plus2 = pltpu.roll(jnp.where(lane < 2, up, v), LANES - 2, 2)
    minus1 = pltpu.roll(jnp.where(lane >= LANES - 1, down, v), 1, 2)
    minus2 = pltpu.roll(jnp.where(lane >= LANES - 2, down, v), 2, 2)
    change = (8.0 / 12.0) * (plus1 - minus1) - (1.0 / 12.0) * (plus2 - minus2)
    return change.reshape(q.shape)


def along_y(q):
    n = q.shape[0] - 4
    near = q[3 : 3 + n] - q[1 : 1 + n]
    far = q[4 : 4 + n] - q[0:n]
    return (8.0 / 12.0) * near - (1.0 / 12.0) * far


def tendency(across, along, q):
    n = q.shape[0] - 4
    return -(across * along_y(q) + along * along_z(q[2 : 2 + n]))


PHASES = ((1, 2), (0,), (3,))


def kernel(
    gx,
    gy,
    ny,
    pieces,
    rounds,
    state,
    kappa,
    out,
    own,
    kap,
    halo,
    kside,
    coef,
    mid,
    vprev,
    qacc,
    sum_m,
    sum_v,
    inv_d,
    track_b,
    track_c,
    take_s,
    take_e,
    edge,
    own_sem,
    near_send,
    near_recv,
    far_send,
    far_recv,
    k_send,
    k_recv,
    m_send,
    m_recv,
    v_send,
    v_recv,
):
    pos = lax.axis_index("gx")
    g = lax.axis_index("gy")
    odd = lax.rem(g, 2)
    partner = g + 1 - 2 * odd
    ahead = lax.rem(g + 2 - 4 * odd + gy, gy)
    behind = lax.rem(g - 2 + 4 * odd + gy, gy)
    nx = kap.shape[0]
    widths = tuple(nx // n for n in pieces)
    tile = kap.shape[1:]
    subs = tile[0] // ny

    barrier = pltpu.get_barrier_semaphore()
    for other in (partner, ahead, behind):
        pl.semaphore_signal(barrier, inc=1, device_id={"gy": other}, device_id_type=MESH)
    for j in range(1, gx):
        pl.semaphore_signal(
            barrier, inc=1, device_id={"gx": lax.rem(pos + j, gx)}, device_id_type=MESH
        )

    def fields_of(ph):
        fields = PHASES[ph]
        return pl.ds(fields[0], len(fields))

    def own_copy(ph):
        f = fields_of(ph)
        return pltpu.make_async_copy(state.at[f], own.at[f], own_sem.at[ph])

    kap_copy = pltpu.make_async_copy(kappa, kap, own_sem.at[3])
    kap_copy.start()
    for ph in range(3):
        own_copy(ph).start()
    pl.semaphore_wait(barrier, 3 + gx - 1)

    def near(ph, c):
        f, part = fields_of(ph), pl.ds(c * widths[ph], widths[ph])
        return pltpu.make_async_remote_copy(
            src_ref=state.at[f, part],
            dst_ref=halo.at[odd, f, part],
            send_sem=near_send.at[ph, c],
            recv_sem=near_recv.at[ph, c],
            device_id={"gy": partner},
            device_id_type=MESH,
        )

    def far(ph, c):
        f, part = fields_of(ph), pl.ds(c * widths[ph], widths[ph])
        return pltpu.make_async_remote_copy(
            src_ref=halo.at[1 - odd, f, part],
            dst_ref=halo.at[odd, f, part],
            send_sem=far_send.at[ph, c],
            recv_sem=far_recv.at[ph, c],
            device_id={"gy": ahead},
            device_id_type=MESH,
        )

    def later(ph, c, by):
        out = []
        start = 0
        for p in range(ph, 3):
            out.append((p, c + by - start, pieces[p]))
            start += pieces[p]
        return out

    def run_later(act, ph, c, by):
        for p, at, count in later(ph, c, by):

            @pl.when((at >= 0) & (at < count))
            def _():
                act(p, at)

    window = 4

    def forward(ph, c):
        near(ph, c).wait_recv()
        far(ph, c).start()
        near(ph, c).wait_send()
        run_later(lambda p, at: near(p, at).start(), ph, c, window)

    def k_copy(to_right):
        side = 0 if to_right else 1
        return pltpu.make_async_remote_copy(
            src_ref=kappa.at[nx - 1 if to_right else 0],
            dst_ref=kside.at[side],
            send_sem=k_send.at[side],
            recv_sem=k_recv.at[side],
            device_id={"gx": lax.rem(pos + (1 if to_right else gx - 1), gx)},
            device_id_type=MESH,
        )

    def bit(k):
        return lax.rem(pos // (2**k), 2)

    def m_copy(k):
        b = bit(k)
        return pltpu.make_async_remote_copy(
            src_ref=sum_m.at[k, b],
            dst_ref=sum_m.at[k, b],
            send_sem=m_send.at[k],
            recv_sem=m_recv.at[k],
            device_id={"gx": pos + (2**k) * (1 - 2 * b)},
            device_id_type=MESH,
        )

    def v_copy(ph, k):
        b = bit(k)
        part = pl.ds(0, 2 * len(PHASES[ph]))
        return pltpu.make_async_remote_copy(
            src_ref=sum_v.at[ph, k, b, part],
            dst_ref=sum_v.at[ph, k, b, part],
            send_sem=v_send.at[ph, k],
            recv_sem=v_recv.at[ph, k],
            device_id={"gx": pos + (2**k) * (1 - 2 * b)},
            device_id_type=MESH,
        )

    @pl.when(pos < gx - 1)
    def _():
        k_copy(True).start()

    @pl.when(pos > 0)
    def _():
        k_copy(False).start()

    for c in range(window):
        run_later(lambda p, at: near(p, at).start(), 0, c, 0)

    zero = jnp.zeros(tile, jnp.float32)
    one = jnp.ones(tile, jnp.float32)
    kap_copy.wait()

    @pl.when(pos > 0)
    def _():
        k_copy(True).wait_recv()

    @pl.when(pos < gx - 1)
    def _():
        k_copy(False).wait_recv()

    @pl.when(pos == 0)
    def _():
        kside[0] = zero

    @pl.when(pos == gx - 1)
    def _():
        kside[1] = zero

    scales = (0.5 * diff_number, 0.5 * diff_number * scalar_ratio)

    def matrix_row(i, k_before, k_here, k_after, carry):
        low_sum = k_before + k_here
        up_sum = k_here + k_after
        new = []
        for m, scale in enumerate(scales):
            slack, w, head_p, head_r = carry[m]
            low = scale * low_sum
            up = scale * up_sum
            excess = 1.0 + low * slack
            inv = 1.0 / (excess + up)
            ratio = up * inv
            linv = low * inv
            w = linv * w
            coef[m, 0, i] = ratio
            coef[m, 1, i] = w
            coef[m, 2, i] = inv
            coef[m, 3, i] = linv
            coef[m, 4, i] = head_p
            new.append((excess * inv, w, head_p * ratio, head_r + head_p * w))
        return tuple(new)

    carry = tuple((one, one, one, zero) for _ in scales)
    carry = matrix_row(0, kside[0], kap[0], kap[1], carry)
    ahead_by = min(3, pieces[0])
    begin = 1
    for c in range(ahead_by + 1):
        until = (nx - 1) * (c + 1) // (ahead_by + 1)
        carry = lax.fori_loop(
            begin,
            until,
            lambda i, cr: matrix_row(i, kap[i - 1], kap[i], kap[i + 1], cr),
            carry,
        )
        begin = until
        if c < ahead_by:
            forward(0, c)
    carry = matrix_row(nx - 1, kap[nx - 2], kap[nx - 1], kside[1], carry)
    for m in range(2):
        _, w, head_p, head_r = carry[m]
        b = bit(0)
        sum_m[0, b, m] = head_p
        sum_m[0, b, 2 + m] = head_r
        sum_m[0, b, 4 + m] = coef[m, 0, nx - 1]
        sum_m[0, b, 6 + m] = w
        track_b[0, m] = one
        track_c[0, m] = zero
        track_b[1, m] = zero
        track_c[1, m] = one
    if rounds:
        m_copy(0).start()

    def merge_matrix(k):
        m_copy(k).wait_recv()
        b = bit(k)
        for m in range(2):
            p1, r1 = sum_m[k, 0, m], sum_m[k, 0, 2 + m]
            last1, w1 = sum_m[k, 0, 4 + m], sum_m[k, 0, 6 + m]
            p2, r2 = sum_m[k, 1, m], sum_m[k, 1, 2 + m]
            last2, w2 = sum_m[k, 1, 4 + m], sum_m[k, 1, 6 + m]
            inv = 1.0 / (1.0 - last1 * r2)
            inv_d[k, m] = inv
            end_b, end_c = w1 * inv, last1 * p2 * inv
            start_b, start_c = r2 * end_b, p2 + r2 * end_c
            if k + 1 < rounds:
                up = bit(k + 1)
                sum_m[k + 1, up, m] = p1 * start_c
                sum_m[k + 1, up, 2 + m] = r1 + p1 * start_b
                sum_m[k + 1, up, 4 + m] = last2 + w2 * end_c
                sum_m[k + 1, up, 6 + m] = w2 * end_b

            @pl.when(b == 0)
            def _():
                for side in range(2):
                    c = track_c[side, m]
                    take_s[k, side, m] = c
                    take_e[k, side, m] = zero
                    track_b[side, m] = track_b[side, m] + c * start_b
                    track_c[side, m] = c * start_c

            @pl.when(b == 1)
            def _():
                for side in range(2):
                    c = track_b[side, m]
                    take_s[k, side, m] = zero
                    take_e[k, side, m] = c
                    track_c[side, m] = track_c[side, m] + c * end_c
                    track_b[side, m] = c * end_b

        if k + 1 < rounds:
            m_copy(k + 1).start()

    def matrix_of(f):
        return 1 if f == 3 else 0

    def start_values(ph):
        b = bit(0)
        for j, f in enumerate(PHASES[ph]):
            sum_v[ph, 0, b, 2 * j] = qacc[f]
            sum_v[ph, 0, b, 2 * j + 1] = vprev[f]
        v_copy(ph, 0).start()

    def merge_values(ph, k):
        v_copy(ph, k).wait_recv()
        for j, f in enumerate(PHASES[ph]):
            m = matrix_of(f)
            q1, v1 = sum_v[ph, k, 0, 2 * j], sum_v[ph, k, 0, 2 * j + 1]
            q2, v2 = sum_v[ph, k, 1, 2 * j], sum_v[ph, k, 1, 2 * j + 1]
            end_a = (v1 + sum_m[k, 0, 4 + m] * q2) * inv_d[k, m]
            start_a = q2 + sum_m[k, 1, 2 + m] * end_a
            if k + 1 < rounds:
                up = bit(k + 1)
                sum_v[ph, k + 1, up, 2 * j] = q1 + sum_m[k, 0, m] * start_a
                sum_v[ph, k + 1, up, 2 * j + 1] = v2 + sum_m[k, 1, 6 + m] * end_a
            for side in range(2):
                edge[side, f] = (
                    edge[side, f] + take_s[k, side, m] * start_a + take_e[k, side, m] * end_a
                )
        if k + 1 < rounds:
            v_copy(ph, k + 1).start()

    def substitute(ph):
        fields = PHASES[ph]
        lefts = tuple(edge[0, f] for f in fields)

        def upward(i, after):
            x = nx - 1 - i
            new = []
            for f, left, nxt in zip(fields, lefts, after):
                m = matrix_of(f)
                here = out[f, x] + coef[m, 1, x] * left + coef[m, 0, x] * nxt
                out[f, x] = here
                new.append(here)
            return tuple(new)

        lax.fori_loop(0, nx, upward, tuple(edge[1, f] for f in fields))

    def rows_of(f, part, reach):
        def row(ref, y):
            return ref[part, pl.ds(y, subs, stride=ny), :]

        return jnp.stack(
            [row(halo.at[0, f], y) for y in range(ny - reach, ny)]
            + [row(own.at[f], y) for y in range(ny)]
            + [row(halo.at[1, f], y) for y in range(reach)]
        )

    def advect(ph, part):
        fields = PHASES[ph]
        wide = [rows_of(f, part, 4) for f in fields]
        if ph == 0:
            across, along = (q[2 : 6 + ny] for q in wide)
        else:
            across, along = rows_of(1, part, 2), rows_of(2, part, 2)
        firsts = [tendency(across, along, q) for q in wide]
        middles = [q[2 : 6 + ny] + step_size * t for q, t in zip(wide, firsts)]
        if ph == 0:
            mid_across, mid_along = (q[2 : 2 + ny] for q in middles)
            mid[0, :, part] = mid_across
            mid[1, :, part] = mid_along
        else:
            mid_across, mid_along = mid[0, :, part], mid[1, :, part]
        for f, q, t, p in zip(fields, wide, firsts, middles):
            second = tendency(mid_across, mid_along, p)
            mixed = q[4 : 4 + ny] + (0.5 * step_size) * (t[2 : 2 + ny] + second)
            for y in range(ny):
                out[f, part, pl.ds(y, subs, stride=ny), :] = mixed[y]

    def eliminate(f, begin):
        m = matrix_of(f)

        def down(j, carry):
            v, q = carry
            x = begin + j
            v = out[f, x] * coef[m, 2, x] + coef[m, 3, x] * v
            out[f, x] = v
            return v, q + coef[m, 4, x] * v

        v, q = lax.fori_loop(0, width, down, (vprev[f], qacc[f]))
        vprev[f] = v
        qacc[f] = q

    for f in range(4):
        vprev[f] = zero
        qacc[f] = zero
        edge[0, f] = zero
        edge[1, f] = zero

    for ph in range(3):
        own_copy(ph).wait()

        chunks, width = pieces[ph], widths[ph]

        @pl.loop(0, chunks)
        def _(c):
            run_later(forward, ph, c, ahead_by)

            for k in range(rounds):
                if ph == 0:

                    @pl.when(c == min(2 * k + 1, chunks - 1))
                    def _():
                        merge_matrix(k)

                else:

                    @pl.when(c == min(2 * k + 2, chunks - 1))
                    def _():
                        merge_values(ph - 1, k)

            if ph > 0:

                @pl.when(c == min(2 * rounds + 2, chunks - 1))
                def _():
                    substitute(ph - 1)

            far(ph, c).wait_recv()

            advect(ph, pl.ds(c * width, width))

            for f in PHASES[ph]:
                eliminate(f, c * width)

        if rounds:
            start_values(ph)

    for k in range(rounds):
        merge_values(2, k)
    substitute(2)

    for ph in range(3):

        @pl.loop(0, pieces[ph])
        def _(c):
            far(ph, c).wait_send()

    @pl.when(pos < gx - 1)
    def _():
        k_copy(True).wait_send()

    @pl.when(pos > 0)
    def _():
        k_copy(False).wait_send()

    for k in range(rounds):
        m_copy(k).wait_send()
        for ph in range(3):
            v_copy(ph, k).wait_send()


def flat(a):
    *lead, ny, nz = a.shape
    a = a.reshape(*lead, ny, nz // LANES, LANES)
    return jnp.swapaxes(a, -3, -2).reshape(*lead, ny * nz // LANES, LANES)


def body(gx, gy, state, diffusivity):
    fields, nx, ny, nz = state.shape
    subs = nz // LANES
    tile = (ny * subs, LANES)
    rounds = gx.bit_length() - 1
    assert gx == 2**rounds and gy % 2 == 0 and ny >= 4
    pieces = tuple(math.gcd(nx, 8 * len(p)) for p in PHASES)
    chunks = max(pieces)
    steps = max(rounds, 1)
    f32 = jnp.float32
    dma = pltpu.SemaphoreType.DMA
    call = pl.pallas_call(
        functools.partial(kernel, gx, gy, ny, pieces, rounds),
        out_shape=jax.ShapeDtypeStruct((fields, nx) + tile, f32),
        in_specs=[pl.BlockSpec(memory_space=pltpu.HBM)] * 2,
        out_specs=pl.BlockSpec(memory_space=pltpu.VMEM),
        scratch_shapes=[
            pltpu.VMEM((fields, nx) + tile, f32),
            pltpu.VMEM((nx,) + tile, f32),
            pltpu.VMEM((2, fields, nx) + tile, f32),
            pltpu.VMEM((2,) + tile, f32),
            pltpu.VMEM((2, 5, nx) + tile, f32),
            pltpu.VMEM((2, ny, nx, subs, LANES), f32),
            pltpu.VMEM((fields,) + tile, f32),
            pltpu.VMEM((fields,) + tile, f32),
            pltpu.VMEM((steps, 2, 8) + tile, f32),
            pltpu.VMEM((3, steps, 2, 4) + tile, f32),
            pltpu.VMEM((steps, 2) + tile, f32),
            pltpu.VMEM((2, 2) + tile, f32),
            pltpu.VMEM((2, 2) + tile, f32),
            pltpu.VMEM((steps, 2, 2) + tile, f32),
            pltpu.VMEM((steps, 2, 2) + tile, f32),
            pltpu.VMEM((2, fields) + tile, f32),
            dma((4,)),
            dma((3, chunks)),
            dma((3, chunks)),
            dma((3, chunks)),
            dma((3, chunks)),
            dma((2,)),
            dma((2,)),
            dma((steps,)),
            dma((steps,)),
            dma((3, steps)),
            dma((3, steps)),
        ],
        compiler_params=pltpu.CompilerParams(
            collective_id=0, has_side_effects=True, vmem_limit_bytes=50 * 2**20
        ),
        cost_estimate=pl.CostEstimate(
            flops=100 * state.size, bytes_accessed=8 * state.size, transcendentals=0
        ),
    )
    result = call(flat(state), flat(diffusivity)).reshape(fields, nx, subs, ny, LANES)
    return jnp.swapaxes(result, -3, -2).reshape(state.shape)


def solution(mesh):
    return jax.shard_map(
        functools.partial(body, mesh.shape["gx"], mesh.shape["gy"]),
        mesh=mesh,
        in_specs=(P(None, "gx", "gy", None), P("gx", "gy", None)),
        out_specs=P(None, "gx", "gy", None),
        check_vma=False,
    )
```

```python
import functools
import math

import jax
import jax.numpy as jnp
from jax import lax
from jax.experimental import pallas as pl
from jax.experimental.pallas import tpu as pltpu
from jax.sharding import PartitionSpec as P

diff_number = 4000.0
scalar_ratio = 1.4
step_size = 0.1
LANES = 128
MESH = pl.DeviceIdType.MESH


def along_z(q):
    v = q.reshape((-1,) + q.shape[-2:])
    lane = lax.broadcasted_iota(jnp.int32, v.shape, 2)
    subs = v.shape[1]
    up = pltpu.roll(v, subs - 1, 1)
    down = pltpu.roll(v, 1, 1)
    plus1 = pltpu.roll(jnp.where(lane < 1, up, v), LANES - 1, 2)
    plus2 = pltpu.roll(jnp.where(lane < 2, up, v), LANES - 2, 2)
    minus1 = pltpu.roll(jnp.where(lane >= LANES - 1, down, v), 1, 2)
    minus2 = pltpu.roll(jnp.where(lane >= LANES - 2, down, v), 2, 2)
    change = (8.0 / 12.0) * (plus1 - minus1) - (1.0 / 12.0) * (plus2 - minus2)
    return change.reshape(q.shape)


def along_y(q):
    n = q.shape[0] - 4
    near = q[3 : 3 + n] - q[1 : 1 + n]
    far = q[4 : 4 + n] - q[0:n]
    return (8.0 / 12.0) * near - (1.0 / 12.0) * far


def tendency(across, along, q):
    n = q.shape[0] - 4
    return -(across * along_y(q) + along * along_z(q[2 : 2 + n]))


PHASES = ((1, 2), (0,), (3,))


def kernel(
    gx,
    gy,
    ny,
    pieces,
    rounds,
    state,
    kappa,
    out,
    own,
    kap,
    halo,
    kside,
    coef,
    mid,
    vprev,
    qacc,
    sum_m,
    sum_v,
    inv_d,
    track_b,
    track_c,
    take_s,
    take_e,
    edge,
    own_sem,
    near_send,
    near_recv,
    far_send,
    far_recv,
    k_send,
    k_recv,
    m_send,
    m_recv,
    v_send,
    v_recv,
):
    pos = lax.axis_index("gx")
    g = lax.axis_index("gy")
    odd = lax.rem(g, 2)
    partner = g + 1 - 2 * odd
    ahead = lax.rem(g + 2 - 4 * odd + gy, gy)
    behind = lax.rem(g - 2 + 4 * odd + gy, gy)
    nx = kap.shape[0]
    widths = tuple(nx // n for n in pieces)
    tile = kap.shape[1:]
    subs = tile[0] // ny

    barrier = pltpu.get_barrier_semaphore()
    for other in (partner, ahead, behind):
        pl.semaphore_signal(barrier, inc=1, device_id={"gy": other}, device_id_type=MESH)
    for j in range(1, gx):
        pl.semaphore_signal(
            barrier, inc=1, device_id={"gx": lax.rem(pos + j, gx)}, device_id_type=MESH
        )

    def fields_of(ph):
        fields = PHASES[ph]
        return pl.ds(fields[0], len(fields))

    def own_copy(ph):
        f = fields_of(ph)
        return pltpu.make_async_copy(state.at[f], own.at[f], own_sem.at[ph])

    kap_copy = pltpu.make_async_copy(kappa, kap, own_sem.at[3])
    kap_copy.start()
    pl.semaphore_wait(barrier, 3 + gx - 1)

    def near(ph, c):
        f, part = fields_of(ph), pl.ds(c * widths[ph], widths[ph])
        return pltpu.make_async_remote_copy(
            src_ref=state.at[f, part],
            dst_ref=halo.at[odd, f, part],
            send_sem=near_send.at[ph, c],
            recv_sem=near_recv.at[ph, c],
            device_id={"gy": partner},
            device_id_type=MESH,
        )

    def far(ph, c):
        f, part = fields_of(ph), pl.ds(c * widths[ph], widths[ph])
        return pltpu.make_async_remote_copy(
            src_ref=halo.at[1 - odd, f, part],
            dst_ref=halo.at[odd, f, part],
            send_sem=far_send.at[ph, c],
            recv_sem=far_recv.at[ph, c],
            device_id={"gy": ahead},
            device_id_type=MESH,
        )

    def later(ph, c, by):
        out = []
        start = 0
        for p in range(ph, 3):
            out.append((p, c + by - start, pieces[p]))
            start += pieces[p]
        return out

    def run_later(act, ph, c, by):
        for p, at, count in later(ph, c, by):

            @pl.when((at >= 0) & (at < count))
            def _():
                act(p, at)

    window = 4

    def forward(ph, c):
        near(ph, c).wait_recv()
        far(ph, c).start()
        near(ph, c).wait_send()
        run_later(lambda p, at: near(p, at).start(), ph, c, window)

    def k_copy(to_right):
        side = 0 if to_right else 1
        return pltpu.make_async_remote_copy(
            src_ref=kappa.at[nx - 1 if to_right else 0],
            dst_ref=kside.at[side],
            send_sem=k_send.at[side],
            recv_sem=k_recv.at[side],
            device_id={"gx": lax.rem(pos + (1 if to_right else gx - 1), gx)},
            device_id_type=MESH,
        )

    def bit(k):
        return lax.rem(pos // (2**k), 2)

    def m_copy(k):
        b = bit(k)
        return pltpu.make_async_remote_copy(
            src_ref=sum_m.at[k, b],
            dst_ref=sum_m.at[k, b],
            send_sem=m_send.at[k],
            recv_sem=m_recv.at[k],
            device_id={"gx": pos + (2**k) * (1 - 2 * b)},
            device_id_type=MESH,
        )

    def v_copy(ph, k):
        b = bit(k)
        part = pl.ds(0, 2 * len(PHASES[ph]))
        return pltpu.make_async_remote_copy(
            src_ref=sum_v.at[ph, k, b, part],
            dst_ref=sum_v.at[ph, k, b, part],
            send_sem=v_send.at[ph, k],
            recv_sem=v_recv.at[ph, k],
            device_id={"gx": pos + (2**k) * (1 - 2 * b)},
            device_id_type=MESH,
        )

    for c in range(window):
        run_later(lambda p, at: near(p, at).start(), 0, c, 0)

    @pl.when(pos < gx - 1)
    def _():
        k_copy(True).start()

    @pl.when(pos > 0)
    def _():
        k_copy(False).start()


    for ph in range(3):
        own_copy(ph).start()

    zero = jnp.zeros(tile, jnp.float32)
    one = jnp.ones(tile, jnp.float32)
    kap_copy.wait()

    @pl.when(pos > 0)
    def _():
        k_copy(True).wait_recv()

    @pl.when(pos < gx - 1)
    def _():
        k_copy(False).wait_recv()

    @pl.when(pos == 0)
    def _():
        kside[0] = zero

    @pl.when(pos == gx - 1)
    def _():
        kside[1] = zero

    scales = (0.5 * diff_number, 0.5 * diff_number * scalar_ratio)

    def matrix_row(i, k_before, k_here, k_after, carry):
        low_sum = k_before + k_here
        up_sum = k_here + k_after
        new = []
        for m, scale in enumerate(scales):
            slack, w, head_p, head_r = carry[m]
            low = scale * low_sum
            up = scale * up_sum
            excess = 1.0 + low * slack
            inv = 1.0 / (excess + up)
            ratio = up * inv
            linv = low * inv
            w = linv * w
            coef[m, 0, i] = ratio
            coef[m, 1, i] = w
            coef[m, 2, i] = inv
            coef[m, 3, i] = linv
            coef[m, 4, i] = head_p
            new.append((excess * inv, w, head_p * ratio, head_r + head_p * w))
        return tuple(new)

    carry = tuple((one, one, one, zero) for _ in scales)
    carry = matrix_row(0, kside[0], kap[0], kap[1], carry)
    ahead_by = min(3, pieces[0])
    begin = 1
    for c in range(ahead_by + 1):
        until = (nx - 1) * (c + 1) // (ahead_by + 1)
        carry = lax.fori_loop(
            begin,
            until,
            lambda i, cr: matrix_row(i, kap[i - 1], kap[i], kap[i + 1], cr),
            carry,
        )
        begin = until
        if c < ahead_by:
            forward(0, c)
    carry = matrix_row(nx - 1, kap[nx - 2], kap[nx - 1], kside[1], carry)
    for m in range(2):
        _, w, head_p, head_r = carry[m]
        b = bit(0)
        sum_m[0, b, m] = head_p
        sum_m[0, b, 2 + m] = head_r
        sum_m[0, b, 4 + m] = coef[m, 0, nx - 1]
        sum_m[0, b, 6 + m] = w
        track_b[0, m] = one
        track_c[0, m] = zero
        track_b[1, m] = zero
        track_c[1, m] = one
    if rounds:
        m_copy(0).start()

    def merge_matrix(k):
        m_copy(k).wait_recv()
        b = bit(k)
        for m in range(2):
            p1, r1 = sum_m[k, 0, m], sum_m[k, 0, 2 + m]
            last1, w1 = sum_m[k, 0, 4 + m], sum_m[k, 0, 6 + m]
            p2, r2 = sum_m[k, 1, m], sum_m[k, 1, 2 + m]
            last2, w2 = sum_m[k, 1, 4 + m], sum_m[k, 1, 6 + m]
            inv = 1.0 / (1.0 - last1 * r2)
            inv_d[k, m] = inv
            end_b, end_c = w1 * inv, last1 * p2 * inv
            start_b, start_c = r2 * end_b, p2 + r2 * end_c
            if k + 1 < rounds:
                up = bit(k + 1)
                sum_m[k + 1, up, m] = p1 * start_c
                sum_m[k + 1, up, 2 + m] = r1 + p1 * start_b
                sum_m[k + 1, up, 4 + m] = last2 + w2 * end_c
                sum_m[k + 1, up, 6 + m] = w2 * end_b

            @pl.when(b == 0)
            def _():
                for side in range(2):
                    c = track_c[side, m]
                    take_s[k, side, m] = c
                    take_e[k, side, m] = zero
                    track_b[side, m] = track_b[side, m] + c * start_b
                    track_c[side, m] = c * start_c

            @pl.when(b == 1)
            def _():
                for side in range(2):
                    c = track_b[side, m]
                    take_s[k, side, m] = zero
                    take_e[k, side, m] = c
                    track_c[side, m] = track_c[side, m] + c * end_c
                    track_b[side, m] = c * end_b

        if k + 1 < rounds:
            m_copy(k + 1).start()

    def matrix_of(f):
        return 1 if f == 3 else 0

    def start_values(ph):
        b = bit(0)
        for j, f in enumerate(PHASES[ph]):
            sum_v[ph, 0, b, 2 * j] = qacc[f]
            sum_v[ph, 0, b, 2 * j + 1] = vprev[f]
        v_copy(ph, 0).start()

    def merge_values(ph, k):
        v_copy(ph, k).wait_recv()
        for j, f in enumerate(PHASES[ph]):
            m = matrix_of(f)
            q1, v1 = sum_v[ph, k, 0, 2 * j], sum_v[ph, k, 0, 2 * j + 1]
            q2, v2 = sum_v[ph, k, 1, 2 * j], sum_v[ph, k, 1, 2 * j + 1]
            end_a = (v1 + sum_m[k, 0, 4 + m] * q2) * inv_d[k, m]
            start_a = q2 + sum_m[k, 1, 2 + m] * end_a
            if k + 1 < rounds:
                up = bit(k + 1)
                sum_v[ph, k + 1, up, 2 * j] = q1 + sum_m[k, 0, m] * start_a
                sum_v[ph, k + 1, up, 2 * j + 1] = v2 + sum_m[k, 1, 6 + m] * end_a
            for side in range(2):
                edge[side, f] = (
                    edge[side, f] + take_s[k, side, m] * start_a + take_e[k, side, m] * end_a
                )
        if k + 1 < rounds:
            v_copy(ph, k + 1).start()

    def substitute(ph):
        fields = PHASES[ph]
        lefts = tuple(edge[0, f] for f in fields)

        def upward(i, after):
            x = nx - 1 - i
            new = []
            for f, left, nxt in zip(fields, lefts, after):
                m = matrix_of(f)
                here = out[f, x] + coef[m, 1, x] * left + coef[m, 0, x] * nxt
                out[f, x] = here
                new.append(here)
            return tuple(new)

        lax.fori_loop(0, nx, upward, tuple(edge[1, f] for f in fields))

    def rows_of(f, part, reach):
        def row(ref, y):
            return ref[part, pl.ds(y, subs, stride=ny), :]

        return jnp.stack(
            [row(halo.at[0, f], y) for y in range(ny - reach, ny)]
            + [row(own.at[f], y) for y in range(ny)]
            + [row(halo.at[1, f], y) for y in range(reach)]
        )

    def advect(ph, part):
        fields = PHASES[ph]
        wide = [rows_of(f, part, 4) for f in fields]
        if ph == 0:
            across, along = (q[2 : 6 + ny] for q in wide)
        else:
            across, along = rows_of(1, part, 2), rows_of(2, part, 2)
        firsts = [tendency(across, along, q) for q in wide]
        middles = [q[2 : 6 + ny] + step_size * t for q, t in zip(wide, firsts)]
        if ph == 0:
            mid_across, mid_along = (q[2 : 2 + ny] for q in middles)
            mid[0, :, part] = mid_across
            mid[1, :, part] = mid_along
        else:
            mid_across, mid_along = mid[0, :, part], mid[1, :, part]
        for f, q, t, p in zip(fields, wide, firsts, middles):
            second = tendency(mid_across, mid_along, p)
            mixed = q[4 : 4 + ny] + (0.5 * step_size) * (t[2 : 2 + ny] + second)
            for y in range(ny):
                out[f, part, pl.ds(y, subs, stride=ny), :] = mixed[y]

    def eliminate(f, begin):
        m = matrix_of(f)

        def down(j, carry):
            v, q = carry
            x = begin + j
            v = out[f, x] * coef[m, 2, x] + coef[m, 3, x] * v
            out[f, x] = v
            return v, q + coef[m, 4, x] * v

        v, q = lax.fori_loop(0, width, down, (vprev[f], qacc[f]))
        vprev[f] = v
        qacc[f] = q

    for f in range(4):
        vprev[f] = zero
        qacc[f] = zero
        edge[0, f] = zero
        edge[1, f] = zero

    for ph in range(3):
        own_copy(ph).wait()

        chunks, width = pieces[ph], widths[ph]

        @pl.loop(0, chunks)
        def _(c):
            run_later(forward, ph, c, ahead_by)

            for k in range(rounds):
                if ph == 0:

                    @pl.when(c == min(2 * k + 1, chunks - 1))
                    def _():
                        merge_matrix(k)

                else:

                    @pl.when(c == min(2 * k + 2, chunks - 1))
                    def _():
                        merge_values(ph - 1, k)

            if ph > 0:

                @pl.when(c == min(2 * rounds + 2, chunks - 1))
                def _():
                    substitute(ph - 1)

            far(ph, c).wait_recv()

            advect(ph, pl.ds(c * width, width))

            for f in PHASES[ph]:
                eliminate(f, c * width)

        if rounds:
            start_values(ph)

    for k in range(rounds):
        merge_values(2, k)
    substitute(2)

    for ph in range(3):

        @pl.loop(0, pieces[ph])
        def _(c):
            far(ph, c).wait_send()

    @pl.when(pos < gx - 1)
    def _():
        k_copy(True).wait_send()

    @pl.when(pos > 0)
    def _():
        k_copy(False).wait_send()

    for k in range(rounds):
        m_copy(k).wait_send()
        for ph in range(3):
            v_copy(ph, k).wait_send()


def flat(a):
    *lead, ny, nz = a.shape
    a = a.reshape(*lead, ny, nz // LANES, LANES)
    return jnp.swapaxes(a, -3, -2).reshape(*lead, ny * nz // LANES, LANES)


def body(gx, gy, state, diffusivity):
    fields, nx, ny, nz = state.shape
    subs = nz // LANES
    tile = (ny * subs, LANES)
    rounds = gx.bit_length() - 1
    assert gx == 2**rounds and gy % 2 == 0 and ny >= 4
    pieces = tuple(math.gcd(nx, 8 * len(p)) for p in PHASES)
    chunks = max(pieces)
    steps = max(rounds, 1)
    f32 = jnp.float32
    dma = pltpu.SemaphoreType.DMA
    call = pl.pallas_call(
        functools.partial(kernel, gx, gy, ny, pieces, rounds),
        out_shape=jax.ShapeDtypeStruct((fields, nx) + tile, f32),
        in_specs=[pl.BlockSpec(memory_space=pltpu.HBM)] * 2,
        out_specs=pl.BlockSpec(memory_space=pltpu.VMEM),
        scratch_shapes=[
            pltpu.VMEM((fields, nx) + tile, f32),
            pltpu.VMEM((nx,) + tile, f32),
            pltpu.VMEM((2, fields, nx) + tile, f32),
            pltpu.VMEM((2,) + tile, f32),
            pltpu.VMEM((2, 5, nx) + tile, f32),
            pltpu.VMEM((2, ny, nx, subs, LANES), f32),
            pltpu.VMEM((fields,) + tile, f32),
            pltpu.VMEM((fields,) + tile, f32),
            pltpu.VMEM((steps, 2, 8) + tile, f32),
            pltpu.VMEM((3, steps, 2, 4) + tile, f32),
            pltpu.VMEM((steps, 2) + tile, f32),
            pltpu.VMEM((2, 2) + tile, f32),
            pltpu.VMEM((2, 2) + tile, f32),
            pltpu.VMEM((steps, 2, 2) + tile, f32),
            pltpu.VMEM((steps, 2, 2) + tile, f32),
            pltpu.VMEM((2, fields) + tile, f32),
            dma((4,)),
            dma((3, chunks)),
            dma((3, chunks)),
            dma((3, chunks)),
            dma((3, chunks)),
            dma((2,)),
            dma((2,)),
            dma((steps,)),
            dma((steps,)),
            dma((3, steps)),
            dma((3, steps)),
        ],
        compiler_params=pltpu.CompilerParams(
            collective_id=0, has_side_effects=True, vmem_limit_bytes=40 * 2**20
        ),
        cost_estimate=pl.CostEstimate(
            flops=100 * state.size, bytes_accessed=8 * state.size, transcendentals=0
        ),
    )
    kap = pltpu.with_memory_space_constraint(flat(diffusivity), pltpu.HBM)
    result = call(pltpu.with_memory_space_constraint(flat(state), pltpu.HBM), kap).reshape(fields, nx, subs, ny, LANES)
    return jnp.swapaxes(result, -3, -2).reshape(state.shape)


def solution(mesh):
    return jax.shard_map(
        functools.partial(body, mesh.shape["gx"], mesh.shape["gy"]),
        mesh=mesh,
        in_specs=(P(None, "gx", "gy", None), P("gx", "gy", None)),
        out_specs=P(None, "gx", "gy", None),
        check_vma=False,
    )
```

```python
import functools
import math

import jax
import jax.numpy as jnp
from jax import lax
from jax.experimental import pallas as pl
from jax.experimental.pallas import tpu as pltpu
from jax.sharding import PartitionSpec as P

diff_number = 4000.0
scalar_ratio = 1.4
step_size = 0.1
LANES = 128
MESH = pl.DeviceIdType.MESH


def along_z(q):
    v = q.reshape((-1,) + q.shape[-2:])
    lane = lax.broadcasted_iota(jnp.int32, v.shape, 2)
    subs = v.shape[1]
    up = pltpu.roll(v, subs - 1, 1)
    down = pltpu.roll(v, 1, 1)
    plus1 = pltpu.roll(jnp.where(lane < 1, up, v), LANES - 1, 2)
    plus2 = pltpu.roll(jnp.where(lane < 2, up, v), LANES - 2, 2)
    minus1 = pltpu.roll(jnp.where(lane >= LANES - 1, down, v), 1, 2)
    minus2 = pltpu.roll(jnp.where(lane >= LANES - 2, down, v), 2, 2)
    change = (8.0 / 12.0) * (plus1 - minus1) - (1.0 / 12.0) * (plus2 - minus2)
    return change.reshape(q.shape)


def along_y(q):
    n = q.shape[0] - 4
    near = q[3 : 3 + n] - q[1 : 1 + n]
    far = q[4 : 4 + n] - q[0:n]
    return (8.0 / 12.0) * near - (1.0 / 12.0) * far


def tendency(across, along, q):
    n = q.shape[0] - 4
    return -(across * along_y(q) + along * along_z(q[2 : 2 + n]))


PHASES = ((1, 2), (0,), (3,))


def kernel(
    gx,
    gy,
    ny,
    pieces,
    rounds,
    state,
    kappa,
    out,
    own,
    kap,
    halo,
    kside,
    coef,
    mid,
    vprev,
    qacc,
    sum_m,
    sum_v,
    inv_d,
    track_b,
    track_c,
    take_s,
    take_e,
    edge,
    own_sem,
    near_send,
    near_recv,
    far_send,
    far_recv,
    k_send,
    k_recv,
    m_send,
    m_recv,
    v_send,
    v_recv,
):
    pos = lax.axis_index("gx")
    g = lax.axis_index("gy")
    odd = lax.rem(g, 2)
    partner = g + 1 - 2 * odd
    ahead = lax.rem(g + 2 - 4 * odd + gy, gy)
    behind = lax.rem(g - 2 + 4 * odd + gy, gy)
    nx = kap.shape[0]
    widths = tuple(nx // n for n in pieces)
    tile = kap.shape[1:]
    subs = tile[0] // ny

    barrier = pltpu.get_barrier_semaphore()
    for other in (partner, ahead, behind):
        pl.semaphore_signal(barrier, inc=1, device_id={"gy": other}, device_id_type=MESH)
    for j in range(1, gx):
        pl.semaphore_signal(
            barrier, inc=1, device_id={"gx": lax.rem(pos + j, gx)}, device_id_type=MESH
        )

    def fields_of(ph):
        fields = PHASES[ph]
        return pl.ds(fields[0], len(fields))

    def own_copy(ph):
        f = fields_of(ph)
        return pltpu.make_async_copy(state.at[f], own.at[f], own_sem.at[ph])

    kap_copy = pltpu.make_async_copy(kappa, kap, own_sem.at[3])
    kap_copy.start()
    pl.semaphore_wait(barrier, 3 + gx - 1)

    def near(ph, c):
        f, part = fields_of(ph), pl.ds(c * widths[ph], widths[ph])
        return pltpu.make_async_remote_copy(
            src_ref=state.at[f, part],
            dst_ref=halo.at[odd, f, part],
            send_sem=near_send.at[ph, c],
            recv_sem=near_recv.at[ph, c],
            device_id={"gy": partner},
            device_id_type=MESH,
        )

    def far(ph, c):
        f, part = fields_of(ph), pl.ds(c * widths[ph], widths[ph])
        return pltpu.make_async_remote_copy(
            src_ref=halo.at[1 - odd, f, part],
            dst_ref=halo.at[odd, f, part],
            send_sem=far_send.at[ph, c],
            recv_sem=far_recv.at[ph, c],
            device_id={"gy": ahead},
            device_id_type=MESH,
        )

    def later(ph, c, by):
        out = []
        start = 0
        for p in range(ph, 3):
            out.append((p, c + by - start, pieces[p]))
            start += pieces[p]
        return out

    def run_later(act, ph, c, by):
        for p, at, count in later(ph, c, by):

            @pl.when((at >= 0) & (at < count))
            def _():
                act(p, at)

    window = 6

    def forward(ph, c):
        near(ph, c).wait_recv()
        far(ph, c).start()
        near(ph, c).wait_send()
        run_later(lambda p, at: near(p, at).start(), ph, c, window)

    def k_copy(to_right):
        side = 0 if to_right else 1
        return pltpu.make_async_remote_copy(
            src_ref=kappa.at[nx - 1 if to_right else 0],
            dst_ref=kside.at[side],
            send_sem=k_send.at[side],
            recv_sem=k_recv.at[side],
            device_id={"gx": lax.rem(pos + (1 if to_right else gx - 1), gx)},
            device_id_type=MESH,
        )

    def bit(k):
        return lax.rem(pos // (2**k), 2)

    def m_copy(k):
        b = bit(k)
        return pltpu.make_async_remote_copy(
            src_ref=sum_m.at[k, b],
            dst_ref=sum_m.at[k, b],
            send_sem=m_send.at[k],
            recv_sem=m_recv.at[k],
            device_id={"gx": pos + (2**k) * (1 - 2 * b)},
            device_id_type=MESH,
        )

    def v_copy(ph, k):
        b = bit(k)
        part = pl.ds(0, 2 * len(PHASES[ph]))
        return pltpu.make_async_remote_copy(
            src_ref=sum_v.at[ph, k, b, part],
            dst_ref=sum_v.at[ph, k, b, part],
            send_sem=v_send.at[ph, k],
            recv_sem=v_recv.at[ph, k],
            device_id={"gx": pos + (2**k) * (1 - 2 * b)},
            device_id_type=MESH,
        )

    for c in range(window):
        run_later(lambda p, at: near(p, at).start(), 0, c, 0)

    @pl.when(pos < gx - 1)
    def _():
        k_copy(True).start()

    @pl.when(pos > 0)
    def _():
        k_copy(False).start()


    for ph in range(3):
        own_copy(ph).start()

    zero = jnp.zeros(tile, jnp.float32)
    one = jnp.ones(tile, jnp.float32)
    kap_copy.wait()

    @pl.when(pos > 0)
    def _():
        k_copy(True).wait_recv()

    @pl.when(pos < gx - 1)
    def _():
        k_copy(False).wait_recv()

    @pl.when(pos == 0)
    def _():
        kside[0] = zero

    @pl.when(pos == gx - 1)
    def _():
        kside[1] = zero

    scales = (0.5 * diff_number, 0.5 * diff_number * scalar_ratio)

    def matrix_row(i, k_before, k_here, k_after, carry):
        low_sum = k_before + k_here
        up_sum = k_here + k_after
        new = []
        for m, scale in enumerate(scales):
            slack, w, head_p, head_r = carry[m]
            low = scale * low_sum
            up = scale * up_sum
            excess = 1.0 + low * slack
            inv = 1.0 / (excess + up)
            ratio = up * inv
            linv = low * inv
            w = linv * w
            coef[m, 0, i] = ratio
            coef[m, 1, i] = w
            coef[m, 2, i] = inv
            coef[m, 3, i] = linv
            coef[m, 4, i] = head_p
            new.append((excess * inv, w, head_p * ratio, head_r + head_p * w))
        return tuple(new)

    carry = tuple((one, one, one, zero) for _ in scales)
    carry = matrix_row(0, kside[0], kap[0], kap[1], carry)
    ahead_by = min(4, pieces[0])
    begin = 1
    for c in range(ahead_by + 1):
        until = (nx - 1) * (c + 1) // (ahead_by + 1)
        carry = lax.fori_loop(
            begin,
            until,
            lambda i, cr: matrix_row(i, kap[i - 1], kap[i], kap[i + 1], cr),
            carry,
        )
        begin = until
        if c < ahead_by:
            forward(0, c)
    carry = matrix_row(nx - 1, kap[nx - 2], kap[nx - 1], kside[1], carry)
    for m in range(2):
        _, w, head_p, head_r = carry[m]
        b = bit(0)
        sum_m[0, b, m] = head_p
        sum_m[0, b, 2 + m] = head_r
        sum_m[0, b, 4 + m] = coef[m, 0, nx - 1]
        sum_m[0, b, 6 + m] = w
        track_b[0, m] = one
        track_c[0, m] = zero
        track_b[1, m] = zero
        track_c[1, m] = one
    if rounds:
        m_copy(0).start()

    def merge_matrix(k):
        m_copy(k).wait_recv()
        b = bit(k)
        for m in range(2):
            p1, r1 = sum_m[k, 0, m], sum_m[k, 0, 2 + m]
            last1, w1 = sum_m[k, 0, 4 + m], sum_m[k, 0, 6 + m]
            p2, r2 = sum_m[k, 1, m], sum_m[k, 1, 2 + m]
            last2, w2 = sum_m[k, 1, 4 + m], sum_m[k, 1, 6 + m]
            inv = 1.0 / (1.0 - last1 * r2)
            inv_d[k, m] = inv
            end_b, end_c = w1 * inv, last1 * p2 * inv
            start_b, start_c = r2 * end_b, p2 + r2 * end_c
            if k + 1 < rounds:
                up = bit(k + 1)
                sum_m[k + 1, up, m] = p1 * start_c
                sum_m[k + 1, up, 2 + m] = r1 + p1 * start_b
                sum_m[k + 1, up, 4 + m] = last2 + w2 * end_c
                sum_m[k + 1, up, 6 + m] = w2 * end_b

            @pl.when(b == 0)
            def _():
                for side in range(2):
                    c = track_c[side, m]
                    take_s[k, side, m] = c
                    take_e[k, side, m] = zero
                    track_b[side, m] = track_b[side, m] + c * start_b
                    track_c[side, m] = c * start_c

            @pl.when(b == 1)
            def _():
                for side in range(2):
                    c = track_b[side, m]
                    take_s[k, side, m] = zero
                    take_e[k, side, m] = c
                    track_c[side, m] = track_c[side, m] + c * end_c
                    track_b[side, m] = c * end_b

        if k + 1 < rounds:
            m_copy(k + 1).start()

    def matrix_of(f):
        return 1 if f == 3 else 0

    def start_values(ph):
        b = bit(0)
        for j, f in enumerate(PHASES[ph]):
            sum_v[ph, 0, b, 2 * j] = qacc[f]
            sum_v[ph, 0, b, 2 * j + 1] = vprev[f]
        v_copy(ph, 0).start()

    def merge_values(ph, k):
        v_copy(ph, k).wait_recv()
        for j, f in enumerate(PHASES[ph]):
            m = matrix_of(f)
            q1, v1 = sum_v[ph, k, 0, 2 * j], sum_v[ph, k, 0, 2 * j + 1]
            q2, v2 = sum_v[ph, k, 1, 2 * j], sum_v[ph, k, 1, 2 * j + 1]
            end_a = (v1 + sum_m[k, 0, 4 + m] * q2) * inv_d[k, m]
            start_a = q2 + sum_m[k, 1, 2 + m] * end_a
            if k + 1 < rounds:
                up = bit(k + 1)
                sum_v[ph, k + 1, up, 2 * j] = q1 + sum_m[k, 0, m] * start_a
                sum_v[ph, k + 1, up, 2 * j + 1] = v2 + sum_m[k, 1, 6 + m] * end_a
            for side in range(2):
                edge[side, f] = (
                    edge[side, f] + take_s[k, side, m] * start_a + take_e[k, side, m] * end_a
                )
        if k + 1 < rounds:
            v_copy(ph, k + 1).start()

    def substitute(ph):
        fields = PHASES[ph]
        lefts = tuple(edge[0, f] for f in fields)

        def upward(i, after):
            x = nx - 1 - i
            new = []
            for f, left, nxt in zip(fields, lefts, after):
                m = matrix_of(f)
                here = out[f, x] + coef[m, 1, x] * left + coef[m, 0, x] * nxt
                out[f, x] = here
                new.append(here)
            return tuple(new)

        lax.fori_loop(0, nx, upward, tuple(edge[1, f] for f in fields))

    def rows_of(f, part, reach):
        def row(ref, y):
            return ref[part, pl.ds(y, subs, stride=ny), :]

        return jnp.stack(
            [row(halo.at[0, f], y) for y in range(ny - reach, ny)]
            + [row(own.at[f], y) for y in range(ny)]
            + [row(halo.at[1, f], y) for y in range(reach)]
        )

    def advect(ph, part):
        fields = PHASES[ph]
        wide = [rows_of(f, part, 4) for f in fields]
        if ph == 0:
            across, along = (q[2 : 6 + ny] for q in wide)
        else:
            across, along = rows_of(1, part, 2), rows_of(2, part, 2)
        firsts = [tendency(across, along, q) for q in wide]
        middles = [q[2 : 6 + ny] + step_size * t for q, t in zip(wide, firsts)]
        if ph == 0:
            mid_across, mid_along = (q[2 : 2 + ny] for q in middles)
            mid[0, :, part] = mid_across
            mid[1, :, part] = mid_along
        else:
            mid_across, mid_along = mid[0, :, part], mid[1, :, part]
        for f, q, t, p in zip(fields, wide, firsts, middles):
            second = tendency(mid_across, mid_along, p)
            mixed = q[4 : 4 + ny] + (0.5 * step_size) * (t[2 : 2 + ny] + second)
            for y in range(ny):
                out[f, part, pl.ds(y, subs, stride=ny), :] = mixed[y]

    def eliminate(f, begin):
        m = matrix_of(f)

        def down(j, carry):
            v, q = carry
            x = begin + j
            v = out[f, x] * coef[m, 2, x] + coef[m, 3, x] * v
            out[f, x] = v
            return v, q + coef[m, 4, x] * v

        v, q = lax.fori_loop(0, width, down, (vprev[f], qacc[f]))
        vprev[f] = v
        qacc[f] = q

    for f in range(4):
        vprev[f] = zero
        qacc[f] = zero
        edge[0, f] = zero
        edge[1, f] = zero

    for ph in range(3):
        own_copy(ph).wait()

        chunks, width = pieces[ph], widths[ph]

        @pl.loop(0, chunks)
        def _(c):
            run_later(forward, ph, c, ahead_by)

            for k in range(rounds):
                if ph == 0:

                    @pl.when(c == min(2 * k + 2, chunks - 1))
                    def _():
                        merge_matrix(k)

                else:

                    @pl.when(c == min(2 * k + 2, chunks - 1))
                    def _():
                        merge_values(ph - 1, k)

            if ph > 0:

                @pl.when(c == min(2 * rounds + 2, chunks - 1))
                def _():
                    substitute(ph - 1)

            far(ph, c).wait_recv()

            advect(ph, pl.ds(c * width, width))

            for f in PHASES[ph]:
                eliminate(f, c * width)

        if rounds:
            start_values(ph)

    for k in range(rounds):
        merge_values(2, k)
    substitute(2)

    for ph in range(3):

        @pl.loop(0, pieces[ph])
        def _(c):
            far(ph, c).wait_send()

    @pl.when(pos < gx - 1)
    def _():
        k_copy(True).wait_send()

    @pl.when(pos > 0)
    def _():
        k_copy(False).wait_send()

    for k in range(rounds):
        m_copy(k).wait_send()
        for ph in range(3):
            v_copy(ph, k).wait_send()


def flat(a):
    *lead, ny, nz = a.shape
    a = a.reshape(*lead, ny, nz // LANES, LANES)
    return jnp.swapaxes(a, -3, -2).reshape(*lead, ny * nz // LANES, LANES)


def body(gx, gy, state, diffusivity):
    fields, nx, ny, nz = state.shape
    subs = nz // LANES
    tile = (ny * subs, LANES)
    rounds = gx.bit_length() - 1
    assert gx == 2**rounds and gy % 2 == 0 and ny >= 4
    pieces = tuple(math.gcd(nx, n) for n in (32, 8, 16))
    chunks = max(pieces)
    steps = max(rounds, 1)
    f32 = jnp.float32
    dma = pltpu.SemaphoreType.DMA
    call = pl.pallas_call(
        functools.partial(kernel, gx, gy, ny, pieces, rounds),
        out_shape=jax.ShapeDtypeStruct((fields, nx) + tile, f32),
        in_specs=[pl.BlockSpec(memory_space=pltpu.HBM)] * 2,
        out_specs=pl.BlockSpec(memory_space=pltpu.VMEM),
        scratch_shapes=[
            pltpu.VMEM((fields, nx) + tile, f32),
            pltpu.VMEM((nx,) + tile, f32),
            pltpu.VMEM((2, fields, nx) + tile, f32),
            pltpu.VMEM((2,) + tile, f32),
            pltpu.VMEM((2, 5, nx) + tile, f32),
            pltpu.VMEM((2, ny, nx, subs, LANES), f32),
            pltpu.VMEM((fields,) + tile, f32),
            pltpu.VMEM((fields,) + tile, f32),
            pltpu.VMEM((steps, 2, 8) + tile, f32),
            pltpu.VMEM((3, steps, 2, 4) + tile, f32),
            pltpu.VMEM((steps, 2) + tile, f32),
            pltpu.VMEM((2, 2) + tile, f32),
            pltpu.VMEM((2, 2) + tile, f32),
            pltpu.VMEM((steps, 2, 2) + tile, f32),
            pltpu.VMEM((steps, 2, 2) + tile, f32),
            pltpu.VMEM((2, fields) + tile, f32),
            dma((4,)),
            dma((3, chunks)),
            dma((3, chunks)),
            dma((3, chunks)),
            dma((3, chunks)),
            dma((2,)),
            dma((2,)),
            dma((steps,)),
            dma((steps,)),
            dma((3, steps)),
            dma((3, steps)),
        ],
        compiler_params=pltpu.CompilerParams(
            collective_id=0, has_side_effects=True, vmem_limit_bytes=40 * 2**20
        ),
        cost_estimate=pl.CostEstimate(
            flops=100 * state.size, bytes_accessed=8 * state.size, transcendentals=0
        ),
    )
    kap = pltpu.with_memory_space_constraint(flat(diffusivity), pltpu.HBM)
    result = call(pltpu.with_memory_space_constraint(flat(state), pltpu.HBM), kap).reshape(fields, nx, subs, ny, LANES)
    return jnp.swapaxes(result, -3, -2).reshape(state.shape)


def solution(mesh):
    return jax.shard_map(
        functools.partial(body, mesh.shape["gx"], mesh.shape["gy"]),
        mesh=mesh,
        in_specs=(P(None, "gx", "gy", None), P("gx", "gy", None)),
        out_specs=P(None, "gx", "gy", None),
        check_vma=False,
    )
```

```python
import functools
import math

import jax
import jax.numpy as jnp
from jax import lax
from jax.experimental import pallas as pl
from jax.experimental.pallas import tpu as pltpu
from jax.sharding import PartitionSpec as P

diff_number = 4000.0
scalar_ratio = 1.4
step_size = 0.1
LANES = 128
MESH = pl.DeviceIdType.MESH


def along_z(q):
    v = q.reshape((-1,) + q.shape[-2:])
    lane = lax.broadcasted_iota(jnp.int32, v.shape, 2)
    subs = v.shape[1]
    up = pltpu.roll(v, subs - 1, 1)
    down = pltpu.roll(v, 1, 1)
    plus1 = pltpu.roll(jnp.where(lane < 1, up, v), LANES - 1, 2)
    plus2 = pltpu.roll(jnp.where(lane < 2, up, v), LANES - 2, 2)
    minus1 = pltpu.roll(jnp.where(lane >= LANES - 1, down, v), 1, 2)
    minus2 = pltpu.roll(jnp.where(lane >= LANES - 2, down, v), 2, 2)
    change = (8.0 / 12.0) * (plus1 - minus1) - (1.0 / 12.0) * (plus2 - minus2)
    return change.reshape(q.shape)


def along_y(q):
    n = q.shape[0] - 4
    near = q[3 : 3 + n] - q[1 : 1 + n]
    far = q[4 : 4 + n] - q[0:n]
    return (8.0 / 12.0) * near - (1.0 / 12.0) * far


def tendency(across, along, q):
    n = q.shape[0] - 4
    return -(across * along_y(q) + along * along_z(q[2 : 2 + n]))


PHASES = ((1, 2), (0,), (3,))


def kernel(
    gx,
    gy,
    ny,
    pieces,
    rounds,
    state,
    kappa,
    out,
    own,
    kap,
    halo,
    kside,
    coef,
    mid,
    speeds,
    vprev,
    qacc,
    sum_m,
    sum_v,
    inv_d,
    track_b,
    track_c,
    take_s,
    take_e,
    edge,
    own_sem,
    near_send,
    near_recv,
    far_send,
    far_recv,
    k_send,
    k_recv,
    m_send,
    m_recv,
    v_send,
    v_recv,
):
    pos = lax.axis_index("gx")
    g = lax.axis_index("gy")
    odd = lax.rem(g, 2)
    partner = g + 1 - 2 * odd
    ahead = lax.rem(g + 2 - 4 * odd + gy, gy)
    behind = lax.rem(g - 2 + 4 * odd + gy, gy)
    nx = kap.shape[0]
    widths = tuple(nx // n for n in pieces)
    tile = kap.shape[1:]
    subs = tile[0] // ny

    barrier = pltpu.get_barrier_semaphore()
    for other in (partner, ahead, behind):
        pl.semaphore_signal(barrier, inc=1, device_id={"gy": other}, device_id_type=MESH)
    for j in range(1, gx):
        pl.semaphore_signal(
            barrier, inc=1, device_id={"gx": lax.rem(pos + j, gx)}, device_id_type=MESH
        )

    def fields_of(ph):
        fields = PHASES[ph]
        return pl.ds(fields[0], len(fields))

    def own_copy(ph):
        f = fields_of(ph)
        return pltpu.make_async_copy(state.at[f], own.at[f], own_sem.at[ph])

    kap_copy = pltpu.make_async_copy(kappa, kap, own_sem.at[3])
    kap_copy.start()
    pl.semaphore_wait(barrier, 3 + gx - 1)

    def near(ph, c):
        f, part = fields_of(ph), pl.ds(c * widths[ph], widths[ph])
        return pltpu.make_async_remote_copy(
            src_ref=state.at[f, part],
            dst_ref=halo.at[odd, f, part],
            send_sem=near_send.at[ph, c],
            recv_sem=near_recv.at[ph, c],
            device_id={"gy": partner},
            device_id_type=MESH,
        )

    def far(ph, c):
        f, part = fields_of(ph), pl.ds(c * widths[ph], widths[ph])
        return pltpu.make_async_remote_copy(
            src_ref=halo.at[1 - odd, f, part],
            dst_ref=halo.at[odd, f, part],
            send_sem=far_send.at[ph, c],
            recv_sem=far_recv.at[ph, c],
            device_id={"gy": ahead},
            device_id_type=MESH,
        )

    def later(ph, c, by):
        out = []
        start = 0
        for p in range(ph, 3):
            out.append((p, c + by - start, pieces[p]))
            start += pieces[p]
        return out

    def run_later(act, ph, c, by):
        for p, at, count in later(ph, c, by):

            @pl.when((at >= 0) & (at < count))
            def _():
                act(p, at)

    window = 4

    def forward(ph, c):
        near(ph, c).wait_recv()
        far(ph, c).start()
        near(ph, c).wait_send()
        run_later(lambda p, at: near(p, at).start(), ph, c, window)

    def k_copy(to_right):
        side = 0 if to_right else 1
        return pltpu.make_async_remote_copy(
            src_ref=kappa.at[nx - 1 if to_right else 0],
            dst_ref=kside.at[side],
            send_sem=k_send.at[side],
            recv_sem=k_recv.at[side],
            device_id={"gx": lax.rem(pos + (1 if to_right else gx - 1), gx)},
            device_id_type=MESH,
        )

    def bit(k):
        return lax.rem(pos // (2**k), 2)

    def m_copy(k):
        b = bit(k)
        return pltpu.make_async_remote_copy(
            src_ref=sum_m.at[k, b],
            dst_ref=sum_m.at[k, b],
            send_sem=m_send.at[k],
            recv_sem=m_recv.at[k],
            device_id={"gx": pos + (2**k) * (1 - 2 * b)},
            device_id_type=MESH,
        )

    def v_copy(ph, k):
        b = bit(k)
        part = pl.ds(0, 2 * len(PHASES[ph]))
        return pltpu.make_async_remote_copy(
            src_ref=sum_v.at[ph, k, b, part],
            dst_ref=sum_v.at[ph, k, b, part],
            send_sem=v_send.at[ph, k],
            recv_sem=v_recv.at[ph, k],
            device_id={"gx": pos + (2**k) * (1 - 2 * b)},
            device_id_type=MESH,
        )

    for c in range(window):
        run_later(lambda p, at: near(p, at).start(), 0, c, 0)

    @pl.when(pos < gx - 1)
    def _():
        k_copy(True).start()

    @pl.when(pos > 0)
    def _():
        k_copy(False).start()


    for ph in range(3):
        own_copy(ph).start()

    zero = jnp.zeros(tile, jnp.float32)
    one = jnp.ones(tile, jnp.float32)
    kap_copy.wait()

    @pl.when(pos > 0)
    def _():
        k_copy(True).wait_recv()

    @pl.when(pos < gx - 1)
    def _():
        k_copy(False).wait_recv()

    @pl.when(pos == 0)
    def _():
        kside[0] = zero

    @pl.when(pos == gx - 1)
    def _():
        kside[1] = zero

    scales = (0.5 * diff_number, 0.5 * diff_number * scalar_ratio)

    def matrix_row(i, k_before, k_here, k_after, carry):
        low_sum = k_before + k_here
        up_sum = k_here + k_after
        new = []
        for m, scale in enumerate(scales):
            slack, w, head_p, head_r = carry[m]
            low = scale * low_sum
            up = scale * up_sum
            excess = 1.0 + low * slack
            inv = 1.0 / (excess + up)
            ratio = up * inv
            linv = low * inv
            w = linv * w
            coef[m, 0, i] = ratio
            coef[m, 1, i] = w
            coef[m, 2, i] = inv
            coef[m, 3, i] = linv
            coef[m, 4, i] = head_p
            new.append((excess * inv, w, head_p * ratio, head_r + head_p * w))
        return tuple(new)

    carry = tuple((one, one, one, zero) for _ in scales)
    carry = matrix_row(0, kside[0], kap[0], kap[1], carry)
    ahead_by = min(3, pieces[0])
    begin = 1
    for c in range(ahead_by + 1):
        until = (nx - 1) * (c + 1) // (ahead_by + 1)
        carry = lax.fori_loop(
            begin,
            until,
            lambda i, cr: matrix_row(i, kap[i - 1], kap[i], kap[i + 1], cr),
            carry,
        )
        begin = until
        if c < ahead_by:
            forward(0, c)
    carry = matrix_row(nx - 1, kap[nx - 2], kap[nx - 1], kside[1], carry)
    for m in range(2):
        _, w, head_p, head_r = carry[m]
        b = bit(0)
        sum_m[0, b, m] = head_p
        sum_m[0, b, 2 + m] = head_r
        sum_m[0, b, 4 + m] = coef[m, 0, nx - 1]
        sum_m[0, b, 6 + m] = w
        track_b[0, m] = one
        track_c[0, m] = zero
        track_b[1, m] = zero
        track_c[1, m] = one
    if rounds:
        m_copy(0).start()

    def merge_matrix(k):
        m_copy(k).wait_recv()
        b = bit(k)
        for m in range(2):
            p1, r1 = sum_m[k, 0, m], sum_m[k, 0, 2 + m]
            last1, w1 = sum_m[k, 0, 4 + m], sum_m[k, 0, 6 + m]
            p2, r2 = sum_m[k, 1, m], sum_m[k, 1, 2 + m]
            last2, w2 = sum_m[k, 1, 4 + m], sum_m[k, 1, 6 + m]
            inv = 1.0 / (1.0 - last1 * r2)
            inv_d[k, m] = inv
            end_b, end_c = w1 * inv, last1 * p2 * inv
            start_b, start_c = r2 * end_b, p2 + r2 * end_c
            if k + 1 < rounds:
                up = bit(k + 1)
                sum_m[k + 1, up, m] = p1 * start_c
                sum_m[k + 1, up, 2 + m] = r1 + p1 * start_b
                sum_m[k + 1, up, 4 + m] = last2 + w2 * end_c
                sum_m[k + 1, up, 6 + m] = w2 * end_b

            @pl.when(b == 0)
            def _():
                for side in range(2):
                    c = track_c[side, m]
                    take_s[k, side, m] = c
                    take_e[k, side, m] = zero
                    track_b[side, m] = track_b[side, m] + c * start_b
                    track_c[side, m] = c * start_c

            @pl.when(b == 1)
            def _():
                for side in range(2):
                    c = track_b[side, m]
                    take_s[k, side, m] = zero
                    take_e[k, side, m] = c
                    track_c[side, m] = track_c[side, m] + c * end_c
                    track_b[side, m] = c * end_b

        if k + 1 < rounds:
            m_copy(k + 1).start()

    def matrix_of(f):
        return 1 if f == 3 else 0

    def start_values(ph):
        b = bit(0)
        for j, f in enumerate(PHASES[ph]):
            sum_v[ph, 0, b, 2 * j] = qacc[f]
            sum_v[ph, 0, b, 2 * j + 1] = vprev[f]
        v_copy(ph, 0).start()

    def merge_values(ph, k):
        v_copy(ph, k).wait_recv()
        for j, f in enumerate(PHASES[ph]):
            m = matrix_of(f)
            q1, v1 = sum_v[ph, k, 0, 2 * j], sum_v[ph, k, 0, 2 * j + 1]
            q2, v2 = sum_v[ph, k, 1, 2 * j], sum_v[ph, k, 1, 2 * j + 1]
            end_a = (v1 + sum_m[k, 0, 4 + m] * q2) * inv_d[k, m]
            start_a = q2 + sum_m[k, 1, 2 + m] * end_a
            if k + 1 < rounds:
                up = bit(k + 1)
                sum_v[ph, k + 1, up, 2 * j] = q1 + sum_m[k, 0, m] * start_a
                sum_v[ph, k + 1, up, 2 * j + 1] = v2 + sum_m[k, 1, 6 + m] * end_a
            for side in range(2):
                edge[side, f] = (
                    edge[side, f] + take_s[k, side, m] * start_a + take_e[k, side, m] * end_a
                )
        if k + 1 < rounds:
            v_copy(ph, k + 1).start()

    def substitute(ph):
        fields = PHASES[ph]
        lefts = tuple(edge[0, f] for f in fields)

        def upward(i, after):
            x = nx - 1 - i
            new = []
            for f, left, nxt in zip(fields, lefts, after):
                m = matrix_of(f)
                here = out[f, x] + coef[m, 1, x] * left + coef[m, 0, x] * nxt
                out[f, x] = here
                new.append(here)
            return tuple(new)

        lax.fori_loop(0, nx, upward, tuple(edge[1, f] for f in fields), unroll=4)

    def rows_of(f, part, reach):
        def row(ref, y):
            return ref[part, pl.ds(y, subs, stride=ny), :]

        return jnp.stack(
            [row(halo.at[0, f], y) for y in range(ny - reach, ny)]
            + [row(own.at[f], y) for y in range(ny)]
            + [row(halo.at[1, f], y) for y in range(reach)]
        )

    def advect(ph, part):
        fields = PHASES[ph]
        wide = [rows_of(f, part, 4) for f in fields]
        if ph == 0:
            across, along = (q[2 : 6 + ny] for q in wide)
            speeds[0, :, part] = across
            speeds[1, :, part] = along
        else:
            across, along = speeds[0, :, part], speeds[1, :, part]
        firsts = [tendency(across, along, q) for q in wide]
        middles = [q[2 : 6 + ny] + step_size * t for q, t in zip(wide, firsts)]
        if ph == 0:
            mid_across, mid_along = (q[2 : 2 + ny] for q in middles)
            mid[0, :, part] = mid_across
            mid[1, :, part] = mid_along
        else:
            mid_across, mid_along = mid[0, :, part], mid[1, :, part]
        for f, q, t, p in zip(fields, wide, firsts, middles):
            second = tendency(mid_across, mid_along, p)
            mixed = q[4 : 4 + ny] + (0.5 * step_size) * (t[2 : 2 + ny] + second)
            for y in range(ny):
                out[f, part, pl.ds(y, subs, stride=ny), :] = mixed[y]

    def eliminate(f, begin):
        m = matrix_of(f)

        def down(j, carry):
            v, q = carry
            x = begin + j
            v = out[f, x] * coef[m, 2, x] + coef[m, 3, x] * v
            out[f, x] = v
            return v, q + coef[m, 4, x] * v

        v, q = lax.fori_loop(0, width, down, (vprev[f], qacc[f]), unroll=True)
        vprev[f] = v
        qacc[f] = q

    for f in range(4):
        vprev[f] = zero
        qacc[f] = zero
        edge[0, f] = zero
        edge[1, f] = zero

    for ph in range(3):
        own_copy(ph).wait()

        chunks, width = pieces[ph], widths[ph]

        @pl.loop(0, chunks)
        def _(c):
            run_later(forward, ph, c, ahead_by)

            for k in range(rounds):
                if ph == 0:

                    @pl.when(c == min(2 * k + 1, chunks - 1))
                    def _():
                        merge_matrix(k)

                else:

                    @pl.when(c == min(2 * k + 2, chunks - 1))
                    def _():
                        merge_values(ph - 1, k)

            if ph > 0:

                @pl.when(c == min(2 * rounds + 2, chunks - 1))
                def _():
                    substitute(ph - 1)

            far(ph, c).wait_recv()

            advect(ph, pl.ds(c * width, width))

            for f in PHASES[ph]:
                eliminate(f, c * width)

        if rounds:
            start_values(ph)

    for k in range(rounds):
        merge_values(2, k)
    substitute(2)

    for ph in range(3):

        @pl.loop(0, pieces[ph])
        def _(c):
            far(ph, c).wait_send()

    @pl.when(pos < gx - 1)
    def _():
        k_copy(True).wait_send()

    @pl.when(pos > 0)
    def _():
        k_copy(False).wait_send()

    for k in range(rounds):
        m_copy(k).wait_send()
        for ph in range(3):
            v_copy(ph, k).wait_send()


def flat(a):
    *lead, ny, nz = a.shape
    a = a.reshape(*lead, ny, nz // LANES, LANES)
    return jnp.swapaxes(a, -3, -2).reshape(*lead, ny * nz // LANES, LANES)


def body(gx, gy, state, diffusivity):
    fields, nx, ny, nz = state.shape
    subs = nz // LANES
    tile = (ny * subs, LANES)
    rounds = gx.bit_length() - 1
    assert gx == 2**rounds and gy % 2 == 0 and ny >= 4
    pieces = tuple(math.gcd(nx, 8 * len(p)) for p in PHASES)
    chunks = max(pieces)
    steps = max(rounds, 1)
    f32 = jnp.float32
    dma = pltpu.SemaphoreType.DMA
    call = pl.pallas_call(
        functools.partial(kernel, gx, gy, ny, pieces, rounds),
        out_shape=jax.ShapeDtypeStruct((fields, nx) + tile, f32),
        in_specs=[pl.BlockSpec(memory_space=pltpu.HBM)] * 2,
        out_specs=pl.BlockSpec(memory_space=pltpu.VMEM),
        scratch_shapes=[
            pltpu.VMEM((fields, nx) + tile, f32),
            pltpu.VMEM((nx,) + tile, f32),
            pltpu.VMEM((2, fields, nx) + tile, f32),
            pltpu.VMEM((2,) + tile, f32),
            pltpu.VMEM((2, 5, nx) + tile, f32),
            pltpu.VMEM((2, ny, nx, subs, LANES), f32),
            pltpu.VMEM((2, ny + 4, nx, subs, LANES), f32),
            pltpu.VMEM((fields,) + tile, f32),
            pltpu.VMEM((fields,) + tile, f32),
            pltpu.VMEM((steps, 2, 8) + tile, f32),
            pltpu.VMEM((3, steps, 2, 4) + tile, f32),
            pltpu.VMEM((steps, 2) + tile, f32),
            pltpu.VMEM((2, 2) + tile, f32),
            pltpu.VMEM((2, 2) + tile, f32),
            pltpu.VMEM((steps, 2, 2) + tile, f32),
            pltpu.VMEM((steps, 2, 2) + tile, f32),
            pltpu.VMEM((2, fields) + tile, f32),
            dma((4,)),
            dma((3, chunks)),
            dma((3, chunks)),
            dma((3, chunks)),
            dma((3, chunks)),
            dma((2,)),
            dma((2,)),
            dma((steps,)),
            dma((steps,)),
            dma((3, steps)),
            dma((3, steps)),
        ],
        compiler_params=pltpu.CompilerParams(
            collective_id=0, has_side_effects=True, vmem_limit_bytes=40 * 2**20
        ),
        cost_estimate=pl.CostEstimate(
            flops=100 * state.size, bytes_accessed=8 * state.size, transcendentals=0
        ),
    )
    kap = pltpu.with_memory_space_constraint(flat(diffusivity), pltpu.HBM)
    result = call(pltpu.with_memory_space_constraint(flat(state), pltpu.HBM), kap).reshape(fields, nx, subs, ny, LANES)
    return jnp.swapaxes(result, -3, -2).reshape(state.shape)


def solution(mesh):
    return jax.shard_map(
        functools.partial(body, mesh.shape["gx"], mesh.shape["gy"]),
        mesh=mesh,
        in_specs=(P(None, "gx", "gy", None), P("gx", "gy", None)),
        out_specs=P(None, "gx", "gy", None),
        check_vma=False,
    )
```

```python
import functools
import math

import jax
import jax.numpy as jnp
from jax import lax
from jax.experimental import pallas as pl
from jax.experimental.pallas import tpu as pltpu
from jax.sharding import PartitionSpec as P

diff_number = 4000.0
scalar_ratio = 1.4
step_size = 0.1
LANES = 128
MESH = pl.DeviceIdType.MESH


def along_z(q):
    v = q.reshape((-1,) + q.shape[-2:])
    lane = lax.broadcasted_iota(jnp.int32, v.shape, 2)
    subs = v.shape[1]
    up = pltpu.roll(v, subs - 1, 1)
    down = pltpu.roll(v, 1, 1)
    plus1 = pltpu.roll(jnp.where(lane < 1, up, v), LANES - 1, 2)
    plus2 = pltpu.roll(jnp.where(lane < 2, up, v), LANES - 2, 2)
    minus1 = pltpu.roll(jnp.where(lane >= LANES - 1, down, v), 1, 2)
    minus2 = pltpu.roll(jnp.where(lane >= LANES - 2, down, v), 2, 2)
    change = (8.0 / 12.0) * (plus1 - minus1) - (1.0 / 12.0) * (plus2 - minus2)
    return change.reshape(q.shape)


def along_y(q):
    n = q.shape[0] - 4
    near = q[3 : 3 + n] - q[1 : 1 + n]
    far = q[4 : 4 + n] - q[0:n]
    return (8.0 / 12.0) * near - (1.0 / 12.0) * far


def tendency(across, along, q):
    n = q.shape[0] - 4
    return -(across * along_y(q) + along * along_z(q[2 : 2 + n]))


PHASES = ((1, 2), (0,), (3,))


def kernel(
    gx,
    gy,
    ny,
    pieces,
    rounds,
    state,
    kappa,
    out,
    own,
    kap,
    halo,
    kside,
    coef,
    mid,
    speeds,
    vprev,
    qacc,
    sum_m,
    sum_v,
    inv_d,
    track_b,
    track_c,
    take_s,
    take_e,
    edge,
    own_sem,
    near_send,
    near_recv,
    far_send,
    far_recv,
    k_send,
    k_recv,
    m_send,
    m_recv,
    v_send,
    v_recv,
):
    pos = lax.axis_index("gx")
    g = lax.axis_index("gy")
    odd = lax.rem(g, 2)
    partner = g + 1 - 2 * odd
    ahead = lax.rem(g + 2 - 4 * odd + gy, gy)
    behind = lax.rem(g - 2 + 4 * odd + gy, gy)
    nx = kap.shape[0]
    widths = tuple(nx // n for n in pieces)
    tile = kap.shape[1:]
    subs = tile[0] // ny

    barrier = pltpu.get_barrier_semaphore()
    for other in (partner, ahead, behind):
        pl.semaphore_signal(barrier, inc=1, device_id={"gy": other}, device_id_type=MESH)
    for j in range(1, gx):
        pl.semaphore_signal(
            barrier, inc=1, device_id={"gx": lax.rem(pos + j, gx)}, device_id_type=MESH
        )

    def fields_of(ph):
        fields = PHASES[ph]
        return pl.ds(fields[0], len(fields))

    def own_copy(ph):
        f = fields_of(ph)
        return pltpu.make_async_copy(state.at[f], own.at[f], own_sem.at[ph])

    kap_copy = pltpu.make_async_copy(kappa, kap, own_sem.at[3])
    kap_copy.start()
    pl.semaphore_wait(barrier, 3 + gx - 1)

    def near(ph, c):
        f, part = fields_of(ph), pl.ds(c * widths[ph], widths[ph])
        return pltpu.make_async_remote_copy(
            src_ref=state.at[f, part],
            dst_ref=halo.at[odd, f, part],
            send_sem=near_send.at[ph, c],
            recv_sem=near_recv.at[ph, c],
            device_id={"gy": partner},
            device_id_type=MESH,
        )

    def far(ph, c):
        f, part = fields_of(ph), pl.ds(c * widths[ph], widths[ph])
        return pltpu.make_async_remote_copy(
            src_ref=halo.at[1 - odd, f, part],
            dst_ref=halo.at[odd, f, part],
            send_sem=far_send.at[ph, c],
            recv_sem=far_recv.at[ph, c],
            device_id={"gy": ahead},
            device_id_type=MESH,
        )

    def later(ph, c, by):
        out = []
        start = 0
        for p in range(ph, 3):
            out.append((p, c + by - start, pieces[p]))
            start += pieces[p]
        return out

    def run_later(act, ph, c, by):
        for p, at, count in later(ph, c, by):

            @pl.when((at >= 0) & (at < count))
            def _():
                act(p, at)

    window = 4

    def forward(ph, c):
        near(ph, c).wait_recv()
        far(ph, c).start()
        near(ph, c).wait_send()
        run_later(lambda p, at: near(p, at).start(), ph, c, window)

    def k_copy(to_right):
        side = 0 if to_right else 1
        return pltpu.make_async_remote_copy(
            src_ref=kappa.at[nx - 1 if to_right else 0],
            dst_ref=kside.at[side],
            send_sem=k_send.at[side],
            recv_sem=k_recv.at[side],
            device_id={"gx": lax.rem(pos + (1 if to_right else gx - 1), gx)},
            device_id_type=MESH,
        )

    def bit(k):
        return lax.rem(pos // (2**k), 2)

    def m_copy(k):
        b = bit(k)
        return pltpu.make_async_remote_copy(
            src_ref=sum_m.at[k, b],
            dst_ref=sum_m.at[k, b],
            send_sem=m_send.at[k],
            recv_sem=m_recv.at[k],
            device_id={"gx": pos + (2**k) * (1 - 2 * b)},
            device_id_type=MESH,
        )

    def v_copy(ph, k):
        b = bit(k)
        part = pl.ds(0, 2 * len(PHASES[ph]))
        return pltpu.make_async_remote_copy(
            src_ref=sum_v.at[ph, k, b, part],
            dst_ref=sum_v.at[ph, k, b, part],
            send_sem=v_send.at[ph, k],
            recv_sem=v_recv.at[ph, k],
            device_id={"gx": pos + (2**k) * (1 - 2 * b)},
            device_id_type=MESH,
        )

    for c in range(window):
        run_later(lambda p, at: near(p, at).start(), 0, c, 0)

    @pl.when(pos < gx - 1)
    def _():
        k_copy(True).start()

    @pl.when(pos > 0)
    def _():
        k_copy(False).start()


    for ph in range(3):
        own_copy(ph).start()

    zero = jnp.zeros(tile, jnp.float32)
    one = jnp.ones(tile, jnp.float32)
    kap_copy.wait()

    @pl.when(pos > 0)
    def _():
        k_copy(True).wait_recv()

    @pl.when(pos < gx - 1)
    def _():
        k_copy(False).wait_recv()

    @pl.when(pos == 0)
    def _():
        kside[0] = zero

    @pl.when(pos == gx - 1)
    def _():
        kside[1] = zero

    scales = (0.5 * diff_number, 0.5 * diff_number * scalar_ratio)

    def matrix_row(i, k_before, k_here, k_after, carry):
        low_sum = k_before + k_here
        up_sum = k_here + k_after
        new = []
        for m, scale in enumerate(scales):
            slack, w, head_p, head_r = carry[m]
            low = scale * low_sum
            up = scale * up_sum
            excess = 1.0 + low * slack
            inv = 1.0 / (excess + up)
            ratio = up * inv
            linv = low * inv
            w = linv * w
            coef[m, 0, i] = ratio
            coef[m, 1, i] = w
            coef[m, 2, i] = inv
            coef[m, 3, i] = linv
            coef[m, 4, i] = head_p
            new.append((excess * inv, w, head_p * ratio, head_r + head_p * w))
        return tuple(new)

    carry = tuple((one, one, one, zero) for _ in scales)
    carry = matrix_row(0, kside[0], kap[0], kap[1], carry)
    ahead_by = min(2, pieces[0])
    begin = 1
    for c in range(ahead_by + 1):
        until = (nx - 1) * (c + 1) // (ahead_by + 1)
        carry = lax.fori_loop(
            begin,
            until,
            lambda i, cr: matrix_row(i, kap[i - 1], kap[i], kap[i + 1], cr),
            carry,
        )
        begin = until
        if c < ahead_by:
            forward(0, c)
    carry = matrix_row(nx - 1, kap[nx - 2], kap[nx - 1], kside[1], carry)
    for m in range(2):
        _, w, head_p, head_r = carry[m]
        b = bit(0)
        sum_m[0, b, m] = head_p
        sum_m[0, b, 2 + m] = head_r
        sum_m[0, b, 4 + m] = coef[m, 0, nx - 1]
        sum_m[0, b, 6 + m] = w
        track_b[0, m] = one
        track_c[0, m] = zero
        track_b[1, m] = zero
        track_c[1, m] = one
    if rounds:
        m_copy(0).start()

    def merge_matrix(k):
        m_copy(k).wait_recv()
        b = bit(k)
        for m in range(2):
            p1, r1 = sum_m[k, 0, m], sum_m[k, 0, 2 + m]
            last1, w1 = sum_m[k, 0, 4 + m], sum_m[k, 0, 6 + m]
            p2, r2 = sum_m[k, 1, m], sum_m[k, 1, 2 + m]
            last2, w2 = sum_m[k, 1, 4 + m], sum_m[k, 1, 6 + m]
            inv = 1.0 / (1.0 - last1 * r2)
            inv_d[k, m] = inv
            end_b, end_c = w1 * inv, last1 * p2 * inv
            start_b, start_c = r2 * end_b, p2 + r2 * end_c
            if k + 1 < rounds:
                up = bit(k + 1)
                sum_m[k + 1, up, m] = p1 * start_c
                sum_m[k + 1, up, 2 + m] = r1 + p1 * start_b
                sum_m[k + 1, up, 4 + m] = last2 + w2 * end_c
                sum_m[k + 1, up, 6 + m] = w2 * end_b

            @pl.when(b == 0)
            def _():
                for side in range(2):
                    c = track_c[side, m]
                    take_s[k, side, m] = c
                    take_e[k, side, m] = zero
                    track_b[side, m] = track_b[side, m] + c * start_b
                    track_c[side, m] = c * start_c

            @pl.when(b == 1)
            def _():
                for side in range(2):
                    c = track_b[side, m]
                    take_s[k, side, m] = zero
                    take_e[k, side, m] = c
                    track_c[side, m] = track_c[side, m] + c * end_c
                    track_b[side, m] = c * end_b

        if k + 1 < rounds:
            m_copy(k + 1).start()

    def matrix_of(f):
        return 1 if f == 3 else 0

    def start_values(ph):
        b = bit(0)
        for j, f in enumerate(PHASES[ph]):
            sum_v[ph, 0, b, 2 * j] = qacc[f]
            sum_v[ph, 0, b, 2 * j + 1] = vprev[f]
        v_copy(ph, 0).start()

    def merge_values(ph, k):
        v_copy(ph, k).wait_recv()
        for j, f in enumerate(PHASES[ph]):
            m = matrix_of(f)
            q1, v1 = sum_v[ph, k, 0, 2 * j], sum_v[ph, k, 0, 2 * j + 1]
            q2, v2 = sum_v[ph, k, 1, 2 * j], sum_v[ph, k, 1, 2 * j + 1]
            end_a = (v1 + sum_m[k, 0, 4 + m] * q2) * inv_d[k, m]
            start_a = q2 + sum_m[k, 1, 2 + m] * end_a
            if k + 1 < rounds:
                up = bit(k + 1)
                sum_v[ph, k + 1, up, 2 * j] = q1 + sum_m[k, 0, m] * start_a
                sum_v[ph, k + 1, up, 2 * j + 1] = v2 + sum_m[k, 1, 6 + m] * end_a
            for side in range(2):
                edge[side, f] = (
                    edge[side, f] + take_s[k, side, m] * start_a + take_e[k, side, m] * end_a
                )
        if k + 1 < rounds:
            v_copy(ph, k + 1).start()

    def substitute(ph):
        fields = PHASES[ph]
        lefts = tuple(edge[0, f] for f in fields)

        def upward(i, after):
            x = nx - 1 - i
            new = []
            for f, left, nxt in zip(fields, lefts, after):
                m = matrix_of(f)
                here = out[f, x] + coef[m, 1, x] * left + coef[m, 0, x] * nxt
                out[f, x] = here
                new.append(here)
            return tuple(new)

        lax.fori_loop(0, nx, upward, tuple(edge[1, f] for f in fields), unroll=4)

    def rows_of(f, part, reach):
        def row(ref, y):
            return ref[part, pl.ds(y, subs, stride=ny), :]

        return jnp.stack(
            [row(halo.at[0, f], y) for y in range(ny - reach, ny)]
            + [row(own.at[f], y) for y in range(ny)]
            + [row(halo.at[1, f], y) for y in range(reach)]
        )

    def advect(ph, part):
        fields = PHASES[ph]
        wide = [rows_of(f, part, 4) for f in fields]
        if ph == 0:
            across, along = (q[2 : 6 + ny] for q in wide)
            speeds[0, :, part] = across
            speeds[1, :, part] = along
        else:
            across, along = speeds[0, :, part], speeds[1, :, part]
        firsts = [tendency(across, along, q) for q in wide]
        middles = [q[2 : 6 + ny] + step_size * t for q, t in zip(wide, firsts)]
        if ph == 0:
            mid_across, mid_along = (q[2 : 2 + ny] for q in middles)
            mid[0, :, part] = mid_across
            mid[1, :, part] = mid_along
        else:
            mid_across, mid_along = mid[0, :, part], mid[1, :, part]
        for f, q, t, p in zip(fields, wide, firsts, middles):
            second = tendency(mid_across, mid_along, p)
            mixed = q[4 : 4 + ny] + (0.5 * step_size) * (t[2 : 2 + ny] + second)
            for y in range(ny):
                out[f, part, pl.ds(y, subs, stride=ny), :] = mixed[y]

    def eliminate(f, begin):
        m = matrix_of(f)

        def down(j, carry):
            v, q = carry
            x = begin + j
            v = out[f, x] * coef[m, 2, x] + coef[m, 3, x] * v
            out[f, x] = v
            return v, q + coef[m, 4, x] * v

        v, q = lax.fori_loop(0, width, down, (vprev[f], qacc[f]), unroll=True)
        vprev[f] = v
        qacc[f] = q

    for f in range(4):
        vprev[f] = zero
        qacc[f] = zero
        edge[0, f] = zero
        edge[1, f] = zero

    for ph in range(3):
        own_copy(ph).wait()

        chunks, width = pieces[ph], widths[ph]

        @pl.loop(0, chunks)
        def _(c):
            run_later(forward, ph, c, ahead_by)

            for k in range(rounds):
                if ph == 0:

                    @pl.when(c == min(2 * k + 1, chunks - 1))
                    def _():
                        merge_matrix(k)

                else:

                    @pl.when(c == min(2 * k + 2, chunks - 1))
                    def _():
                        merge_values(ph - 1, k)

            if ph > 0:

                @pl.when(c == min(2 * rounds + 2, chunks - 1))
                def _():
                    substitute(ph - 1)

            far(ph, c).wait_recv()

            advect(ph, pl.ds(c * width, width))

            for f in PHASES[ph]:
                eliminate(f, c * width)

        if rounds:
            start_values(ph)

    for k in range(rounds):
        merge_values(2, k)
    substitute(2)

    for ph in range(3):

        @pl.loop(0, pieces[ph])
        def _(c):
            far(ph, c).wait_send()

    @pl.when(pos < gx - 1)
    def _():
        k_copy(True).wait_send()

    @pl.when(pos > 0)
    def _():
        k_copy(False).wait_send()

    for k in range(rounds):
        m_copy(k).wait_send()
        for ph in range(3):
            v_copy(ph, k).wait_send()


def flat(a):
    *lead, ny, nz = a.shape
    a = a.reshape(*lead, ny, nz // LANES, LANES)
    return jnp.swapaxes(a, -3, -2).reshape(*lead, ny * nz // LANES, LANES)


def body(gx, gy, state, diffusivity):
    fields, nx, ny, nz = state.shape
    subs = nz // LANES
    tile = (ny * subs, LANES)
    rounds = gx.bit_length() - 1
    assert gx == 2**rounds and gy % 2 == 0 and ny >= 4
    pieces = tuple(math.gcd(nx, 8) for p in PHASES)
    chunks = max(pieces)
    steps = max(rounds, 1)
    f32 = jnp.float32
    dma = pltpu.SemaphoreType.DMA
    call = pl.pallas_call(
        functools.partial(kernel, gx, gy, ny, pieces, rounds),
        out_shape=jax.ShapeDtypeStruct((fields, nx) + tile, f32),
        in_specs=[pl.BlockSpec(memory_space=pltpu.HBM)] * 2,
        out_specs=pl.BlockSpec(memory_space=pltpu.VMEM),
        scratch_shapes=[
            pltpu.VMEM((fields, nx) + tile, f32),
            pltpu.VMEM((nx,) + tile, f32),
            pltpu.VMEM((2, fields, nx) + tile, f32),
            pltpu.VMEM((2,) + tile, f32),
            pltpu.VMEM((2, 5, nx) + tile, f32),
            pltpu.VMEM((2, ny, nx, subs, LANES), f32),
            pltpu.VMEM((2, ny + 4, nx, subs, LANES), f32),
            pltpu.VMEM((fields,) + tile, f32),
            pltpu.VMEM((fields,) + tile, f32),
            pltpu.VMEM((steps, 2, 8) + tile, f32),
            pltpu.VMEM((3, steps, 2, 4) + tile, f32),
            pltpu.VMEM((steps, 2) + tile, f32),
            pltpu.VMEM((2, 2) + tile, f32),
            pltpu.VMEM((2, 2) + tile, f32),
            pltpu.VMEM((steps, 2, 2) + tile, f32),
            pltpu.VMEM((steps, 2, 2) + tile, f32),
            pltpu.VMEM((2, fields) + tile, f32),
            dma((4,)),
            dma((3, chunks)),
            dma((3, chunks)),
            dma((3, chunks)),
            dma((3, chunks)),
            dma((2,)),
            dma((2,)),
            dma((steps,)),
            dma((steps,)),
            dma((3, steps)),
            dma((3, steps)),
        ],
        compiler_params=pltpu.CompilerParams(
            collective_id=0, has_side_effects=True, vmem_limit_bytes=40 * 2**20
        ),
        cost_estimate=pl.CostEstimate(
            flops=100 * state.size, bytes_accessed=8 * state.size, transcendentals=0
        ),
    )
    kap = pltpu.with_memory_space_constraint(flat(diffusivity), pltpu.HBM)
    result = call(pltpu.with_memory_space_constraint(flat(state), pltpu.HBM), kap).reshape(fields, nx, subs, ny, LANES)
    return jnp.swapaxes(result, -3, -2).reshape(state.shape)


def solution(mesh):
    return jax.shard_map(
        functools.partial(body, mesh.shape["gx"], mesh.shape["gy"]),
        mesh=mesh,
        in_specs=(P(None, "gx", "gy", None), P("gx", "gy", None)),
        out_specs=P(None, "gx", "gy", None),
        check_vma=False,
    )
```
